256 devices in a mesh: tile: 8 (over z), pos: 32 (over x, y, core).
Axes of the slice: x: 4, y: 4, z: 8, core: 2. Of those that a mesh axis runs over, the one named last changes fastest.
Arguments:
- object_field: float32 [2, 512, 4096], P(None, 'pos', 'tile'), may hold values from -6 to 6
- illumination: float32 [2, 128, 128], replicated, may hold values from -6 to 6
- row_offsets: int32 [2, 8192], P(None, ('tile', 'pos')), may hold values from 0 to 384
- col_offsets: int32 [2, 8192], P(None, ('tile', 'pos')), may hold values from 0 to 384
- counts: int32 [2, 256], P(None, ('tile', 'pos')), may hold values from 1 to 32, as said below
- amplitudes: float32 [2, 8192, 128, 128], P(None, ('tile', 'pos')), may hold values from 0.05 to 4
Outputs:
- object_out: float32 [2, 512, 4096], P(None, 'pos', 'tile')
- probe_out: float32 [2, 128, 128], replicated
The draws below stay inside these ranges and needn't reach their ends.
Inputs may be any that keep to these rules, and one draw needn't show every extreme that they name: `counts`: in every iteration, in every strip, one device has exactly 32 live slots; a device's live slots are its first ones.
All inputs are finite; a program needn't handle non-finite values.
Results may differ from the reference program's by a relative error of at most 0.0003.
Values sent between devices are 32-bit elements; how exact they have to be, the bound alone decides.
A program may use at most 128 MiB of HBM per device.

```python
import math
import jax
import jax.numpy as jnp
from jax import lax

WIN = 128
ROWS = 512
STRIP = 512
CAP = 32
ITERS = 2
NCOLS = 4096
SLOTS = 8192
N_TILE = 8
N_POS = 32


def draw_counts(key, part):
    key = jax.random.fold_in(key, 11)
    first_key, second_key = jax.random.split(key)
    baseline = jax.random.randint(first_key, (ITERS, N_TILE, N_POS), 1, 2 * CAP // 3 + 1)
    busiest = jax.random.randint(second_key, (ITERS, N_TILE, 1), 0, N_POS)
    member_rank = lax.broadcasted_iota(jnp.int32, (ITERS, N_TILE, N_POS), 2)
    filled = jnp.where(member_rank == busiest, CAP, baseline)
    return filled.reshape(ITERS, N_TILE * N_POS).astype(jnp.int32)


def touch_ends(entries, key, low, largest):
    place = [jax.random.randint(jax.random.fold_in(key, axis), (), 0, length) for axis, length in enumerate(entries.shape)]
    main_axis = entries.shape.index(max(entries.shape))
    neighbour = place[:main_axis] + [(place[main_axis] + 1) % entries.shape[main_axis]] + place[main_axis + 1:]
    return entries.at[tuple(place)].set(low).at[tuple(neighbour)].set(largest)


def levels(key, dims, pieces, smallest, high):
    level, own = 1.0, jax.random.fold_in(key, 6)
    for position, shards_of in pieces:
        draws = jnp.exp(jax.random.uniform(jax.random.fold_in(own, position), (shards_of,), jnp.float32, smallest / len(pieces), high / len(pieces)))
        level = level * jnp.repeat(draws, dims[position] // shards_of).reshape([-1 if axis == position else 1 for axis in range(len(dims))])
    return level


def noise(rng, extent, scale, limit, cuts=(), kind=jnp.bfloat16):
    entries = scale * jax.random.normal(rng, extent, jnp.float32)
    if cuts:
        entries = entries * levels(rng, extent, cuts, -0.22, 0.18)
    return jnp.clip(entries, -limit, limit).astype(kind)


def setup_inputs(seed: int = 0) -> dict:
    splits = jax.random.split(jax.random.key(seed), 7)
    return {
        "object_field": noise(splits[0], (2, ROWS, NCOLS), 1.0, 6.0, ((1, 32), (2, 8)), jnp.float32),
        "illumination": noise(splits[1], (2, WIN, WIN), 1.0, 6.0, (), jnp.float32),
        "row_offsets": touch_ends(jax.random.randint(splits[2], (ITERS, SLOTS), 0, ROWS - WIN + 1), jax.random.fold_in(splits[2], 1), 0, ROWS - WIN).astype(jnp.int32),
        "col_offsets": touch_ends(jax.random.randint(splits[3], (ITERS, SLOTS), 0, STRIP - WIN + 1), jax.random.fold_in(splits[3], 1), 0, STRIP - WIN).astype(jnp.int32),
        "counts": draw_counts(jax.random.fold_in(splits[6], 71), 0),
        "amplitudes": jnp.clip(jnp.exp(math.log(4.0) - 4.3820266 * jax.random.uniform(splits[5], (ITERS, SLOTS, WIN, WIN), jnp.float32) ** levels(splits[5], (ITERS, SLOTS, WIN, WIN), ((1, 256),), -0.2, 0.2)), 0.05, 4.0),
    }


def slot_terms(object_strip, illumination, row_start, col_start, measured):
    width = illumination.shape[-1]
    anchor = jnp.zeros((), jnp.int32)
    patch = lax.dynamic_slice(object_strip, (anchor, row_start, col_start), (2, width, width))
    patch_real, patch_imag = (patch[0], patch[1])
    probe_real, probe_imag = (illumination[0], illumination[1])
    exit_real = probe_real * patch_real - probe_imag * patch_imag
    exit_imag = probe_real * patch_imag + probe_imag * patch_real
    far_field = jnp.fft.fft2(lax.complex(exit_real, exit_imag), norm='ortho')
    far_real = jnp.real(far_field)
    far_imag = jnp.imag(far_field)
    modulus = jnp.sqrt(far_real * far_real + far_imag * far_imag + 1.0)
    factor = measured / modulus - 1.0
    back_field = jnp.fft.ifft2(lax.complex(far_real * factor, far_imag * factor), norm='ortho')
    back_real = jnp.real(back_field)
    back_imag = jnp.imag(back_field)
    object_terms = jnp.stack([probe_real * back_real + probe_imag * back_imag, probe_real * back_imag - probe_imag * back_real, probe_real * probe_real + probe_imag * probe_imag])
    probe_terms = jnp.stack([patch_real * back_real + patch_imag * back_imag, patch_real * back_imag - patch_imag * back_real, patch_real * patch_real + patch_imag * patch_imag])
    return (object_terms, probe_terms)

def reference(object_field, illumination, row_offsets, col_offsets, counts, amplitudes):
    group_slots = N_POS * CAP
    anchor = jnp.zeros((), jnp.int32)
    for iteration in range(ITERS):
        probe_sums = jnp.zeros((3, WIN, WIN), jnp.float32)
        strips = []
        for tile_number in range(N_TILE):
            object_strip = object_field[:, :, tile_number * STRIP:(tile_number + 1) * STRIP]
            first_slot = tile_number * group_slots
            row_starts = row_offsets[iteration, first_slot:first_slot + group_slots]
            col_starts = col_offsets[iteration, first_slot:first_slot + group_slots]
            measured = amplitudes[iteration, first_slot:first_slot + group_slots]
            local_slot = jnp.arange(group_slots, dtype=jnp.int32) % CAP
            limits = jnp.repeat(counts[iteration, tile_number * N_POS:(tile_number + 1) * N_POS], CAP)
            alive_flags = local_slot < limits

            def visit(carry, slot_data):
                row_start, col_start, slot_amplitude, alive = slot_data

                def busy(state):
                    totals, sums = state
                    object_terms, probe_terms = slot_terms(object_strip, illumination, row_start, col_start, slot_amplitude)
                    current = lax.dynamic_slice(totals, (anchor, row_start, col_start), (3, WIN, WIN))
                    totals = lax.dynamic_update_slice(totals, current + object_terms, (anchor, row_start, col_start))
                    return (totals, sums + probe_terms)

                def unchanged(state):
                    return state
                return (lax.cond(alive, busy, unchanged, carry), None)
            start_totals = jnp.zeros((3, ROWS, STRIP), jnp.float32)
            (totals, probe_sums), _ = lax.scan(visit, (start_totals, probe_sums), (row_starts, col_starts, measured, alive_flags))
            strips.append(object_strip + totals[:2] / (totals[2] + 1.0))
        object_field = jnp.concatenate(strips, axis=2)
        illumination = illumination + probe_sums[:2] / jnp.sqrt(probe_sums[2] + 1.0)
    return (object_field, illumination)
```

```python
import functools
import math

import jax
import jax.numpy as jnp
import ml_dtypes
import numpy as np
from jax import lax
from jax.experimental import pallas as pl
from jax.experimental.pallas import tpu as pltpu
from jax.sharding import PartitionSpec as P

WIN = 128
ROWS = 512
GROUPS = ROWS // 8
COLS = ROWS // WIN
PTILES = 3 * WIN // 8
BLOCK = 4
RING = 4
MESH = pl.DeviceIdType.MESH
f32 = jnp.float32


def transform_tables():
    ramp = np.arange(WIN)
    angle = -2.0 * np.pi / WIN * (np.outer(ramp, ramp) % WIN)
    c, s = np.cos(angle) / math.sqrt(WIN), np.sin(angle) / math.sqrt(WIN)
    pairs = []
    for matrix in (np.block([[c, s], [-s, c]]), np.block([[c, -s], [s, c]])):
        high = matrix.astype(ml_dtypes.bfloat16)
        low = (matrix - high.astype(np.float64)).astype(ml_dtypes.bfloat16)
        pairs.append((high, low))
    (ah, al), (bh, bl) = pairs
    right = np.stack([np.concatenate([ah, ah, al]), np.concatenate([bh, bh, bl])])
    left = np.stack([np.concatenate([bh, bh, bl], 1), np.concatenate([ah, ah, al], 1)])
    return right, left


def split(x):
    high = x.astype(jnp.bfloat16)
    return high, (x - high.astype(f32)).astype(jnp.bfloat16)


def transform(pairs, right, left):
    halves = [[split(part) for part in pair] for pair in pairs]
    high, low = (
        jnp.concatenate([jnp.concatenate([re[k], im[k]], 1) for re, im in halves], 0) for k in range(2)
    )
    y = jnp.dot(jnp.concatenate([high, low, high], 1), right, preferred_element_type=f32)
    out = []
    for k in range(0, len(pairs), 2):
        quarters = [
            [split(y[(k + j) * WIN : (k + j + 1) * WIN, p * WIN : (p + 1) * WIN]) for j in range(2)]
            for p in range(2)
        ]
        high, low = (
            jnp.concatenate([jnp.concatenate([q[n] for q in row], 1) for row in quarters], 0) for n in range(2)
        )
        z = jnp.dot(left, jnp.concatenate([high, low, high], 0), preferred_element_type=f32)
        for j in range(2):
            out.append((z[:WIN, j * WIN : (j + 1) * WIN], z[WIN:, j * WIN : (j + 1) * WIN]))
    return out


def probe_step(probe, sums):
    scale = lax.rsqrt(sums[2] + 1.0)
    return [probe[k] + (sums[k] - probe[k] * sums[2]) * scale for k in range(2)]


def sweep_kernel(
    iteration, rows_hbm, cols_hbm, counts_hbm, probe_hbm, right_hbm, left_hbm, strip_hbm, amp_hbm,
    out_hbm, probe_out,
    rows, cols, counts, right, left, probe, old_sums, strip, sums, amp, probe_sums, small_sem, strip_sem, amp_sem, out_sem,
):
    cap = rows.shape[1]
    n_blocks = cap // BLOCK
    updates = strip_hbm.shape[1] > 2 * COLS
    copies = [
        pltpu.make_async_copy(src, dst, small_sem.at[k])
        for k, (src, dst) in enumerate(
            [(counts_hbm, counts), (rows_hbm, rows), (cols_hbm, cols), (probe_hbm, probe), (right_hbm, right), (left_hbm, left)]
        )
    ]
    if updates:
        copies.append(pltpu.make_async_copy(strip_hbm.at[pl.ds(0, PTILES), 2 * COLS], old_sums, small_sem.at[6]))
    copies += [pltpu.make_async_copy(strip_hbm.at[:, k], strip.at[k], strip_sem.at[k]) for k in range(2 * COLS)]
    for copy in copies:
        copy.start()

    def amp_copy(k):
        part = pl.ds(k * BLOCK, BLOCK)
        return pltpu.make_async_copy(amp_hbm.at[iteration, part], amp.at[part], amp_sem.at[k])

    for k in range(n_blocks):
        amp_copy(k).start()
    sums_rows = sums.reshape(3 * COLS, ROWS, WIN)
    strip_rows = strip.reshape(2 * COLS, ROWS, WIN)
    probe_rows = probe_sums.reshape(ROWS // WIN, WIN, WIN)
    for k in range(3 * COLS):
        sums_rows[k] = jnp.zeros((ROWS, WIN), f32)
    for k in range(ROWS // WIN):
        probe_rows[k] = jnp.zeros((WIN, WIN), f32)
    for copy in copies:
        copy.wait()
    if updates:
        stepped = probe_step(probe, old_sums.reshape(3, WIN, WIN))
        for k in range(2):
            probe[k] = stepped[k]
    probe_out[...] = probe[...]
    count = counts[iteration, 0]
    lane = lax.broadcasted_iota(jnp.int32, (WIN, WIN), 1)
    trips = (count + BLOCK - 1) // BLOCK

    def body(k, carry):
        amp_copy(k).wait()
        held, exits = [], []
        for j in range(BLOCK):
            slot = k * BLOCK + j
            row, col = rows[iteration, slot], cols[iteration, slot]
            first, turn = col // WIN, col % WIN
            second = jnp.minimum(first + 1, COLS - 1)
            here = lane >= turn
            window = pl.ds(row, WIN)
            q = [
                jnp.where(here, strip_rows[COLS * p + first, window, :], strip_rows[COLS * p + second, window, :])
                for p in range(2)
            ]
            pr = [pltpu.roll(probe[p], turn, 1) for p in range(2)]
            exits.append((pr[0] * q[0] - pr[1] * q[1], pr[0] * q[1] + pr[1] * q[0]))
            held.append((slot, window, first, second, turn, here, q, pr))
        scaled = []
        for (slot, *_), (re, im) in zip(held, transform(exits, right[0], left[0])):
            factor = amp[slot] * lax.rsqrt(re * re + im * im + 1.0)
            factor = jnp.where(slot < count, factor, 0.0)
            scaled.append((re * factor, im * factor))
        for (slot, window, first, second, turn, here, (qr, qi), (pr, pi)), (gr, gi) in zip(
            held, transform(scaled, right[1], left[1])
        ):
            live = (slot < count).astype(f32)
            for p, term in enumerate((pr * gr + pi * gi, pr * gi - pi * gr, (pr * pr + pi * pi) * live)):
                sums_rows[COLS * p + first, window, :] += jnp.where(here, term, 0.0)
                sums_rows[COLS * p + second, window, :] += jnp.where(here, 0.0, term)
            back = jnp.where(turn == 0, 0, WIN - turn)
            for p, term in enumerate((qr * gr + qi * gi, qr * gi - qi * gr, (qr * qr + qi * qi) * live)):
                probe_rows[p] += pltpu.roll(term, back, 1)
        return carry

    lax.fori_loop(0, trips, body, 0)

    def drain(k, carry):
        amp_copy(k).wait()
        return carry

    lax.fori_loop(trips, n_blocks, drain, 0)
    outs = [pltpu.make_async_copy(sums.at[k], out_hbm.at[:, k], out_sem.at[k]) for k in range(3 * COLS)]
    outs.append(pltpu.make_async_copy(probe_sums, out_hbm.at[:, 3 * COLS], out_sem.at[3 * COLS]))
    for copy in outs:
        copy.start()
    for copy in outs:
        copy.wait()


ANY = pl.BlockSpec(memory_space=pl.ANY)
VMEM = pl.BlockSpec(memory_space=pltpu.VMEM)


def sweep(iteration, strip, probe, rows, cols, counts, amplitudes, right, left):
    cap = rows.shape[1]
    return pl.pallas_call(
        functools.partial(sweep_kernel, iteration),
        out_shape=(
            jax.ShapeDtypeStruct((GROUPS, 3 * COLS + 1, 8, WIN), f32),
            jax.ShapeDtypeStruct(probe.shape, f32),
        ),
        in_specs=[ANY] * 8,
        out_specs=(ANY, VMEM),
        scratch_shapes=[
            pltpu.SMEM(rows.shape, jnp.int32),
            pltpu.SMEM(cols.shape, jnp.int32),
            pltpu.SMEM(counts.shape, jnp.int32),
            pltpu.VMEM(right.shape, jnp.bfloat16),
            pltpu.VMEM(left.shape, jnp.bfloat16),
            pltpu.VMEM(probe.shape, f32),
            pltpu.VMEM((PTILES, 8, WIN), f32),
            pltpu.VMEM((2 * COLS, GROUPS, 8, WIN), f32),
            pltpu.VMEM((3 * COLS, GROUPS, 8, WIN), f32),
            pltpu.VMEM((cap, WIN, WIN), f32),
            pltpu.VMEM((GROUPS, 8, WIN), f32),
            pltpu.SemaphoreType.DMA((7,)),
            pltpu.SemaphoreType.DMA((2 * COLS,)),
            pltpu.SemaphoreType.DMA((cap // BLOCK,)),
            pltpu.SemaphoreType.DMA((3 * COLS + 1,)),
        ],
        compiler_params=pltpu.CompilerParams(vmem_limit_bytes=40 * 1024 * 1024),
        name="sweep",
    )(rows, cols, counts, probe, right, left, strip, amplitudes)


class Place:
    def __init__(self):
        pos = lax.axis_index("pos")
        self.tile = lax.axis_index("tile")
        core, y, x = pos % 2, pos // 2 % RING, pos // (2 * RING)
        self.core = core
        self.near, self.far = x + core * (y - x), y + core * (x - y)
        self.near_step, self.far_step = 8 - 6 * core, 2 + 6 * core

    def at(self, near, far):
        return (self.near + near) % RING * self.near_step + (self.far + far) % RING * self.far_step + self.core

    def other_at(self, near, far):
        return (self.far + near) % RING * self.far_step + (self.near + far) % RING * self.near_step + 1 - self.core

    def partners(self):
        return [self.at(1, 0), self.at(3, 0), self.at(0, 1), self.at(0, 3), self.other_at(0, 0)]


def greet(place, with_tiles):
    barrier = pltpu.get_barrier_semaphore()
    for partner in place.partners():
        pl.semaphore_signal(barrier, inc=1, device_id={"pos": partner}, device_id_type=MESH)
    tiles = lax.axis_size("tile") if with_tiles else 1
    for k in range(1, tiles):
        pl.semaphore_signal(barrier, inc=1, device_id={"tile": (place.tile + k) % tiles}, device_id_type=MESH)
    pl.semaphore_wait(barrier, len(place.partners()) + tiles - 1)


class Sender:
    def __init__(self, send_sem, recv_sem):
        self.send_sem, self.recv_sem = send_sem, recv_sem
        self.names, self.sent = {}, []

    def slot(self, name):
        return self.names.setdefault(name, len(self.names))

    def copy(self, name, src, dst, device):
        k = self.slot(name)
        return pltpu.make_async_remote_copy(
            src_ref=src, dst_ref=dst, send_sem=self.send_sem.at[k], recv_sem=self.recv_sem.at[k],
            device_id=device, device_id_type=MESH,
        )

    def send(self, name, src, dst, device):
        copy = self.copy(name, src, dst, device)
        copy.start()
        self.sent.append(copy)

    def arrive(self, name, dst, device):
        self.copy(name, dst, dst, device).wait_recv()

    def finish(self):
        for copy in self.sent:
            copy.wait_send()


def gather(place, sender, buf):
    np_, nm, fp, fm, other = [{"pos": p} for p in place.partners()]

    def both(near, far):
        return buf.at[pl.ds(2 * place.at(near, far), 2)]

    def half(near, far, k):
        return buf.at[2 * place.at(near, far) + k]

    def pass_on(near):
        sender.send(("f+", near), both(near, 0), both(near, 0), fp)
        sender.send(("f-", near), both(near, 0), both(near, 0), fm)

    def to_other(near, far):
        sender.send(("core", near, far), both(near, far), both(near, far), other)

    sender.send("n+", both(0, 0), both(0, 0), np_)
    sender.send("n-", both(0, 0), both(0, 0), nm)
    pass_on(0)
    to_other(0, 0)
    sender.arrive("n+", both(3, 0), nm)
    sender.send("n++", half(3, 0, 0), half(3, 0, 0), np_)
    pass_on(3)
    sender.arrive("n-", both(1, 0), np_)
    sender.send("n--", half(1, 0, 1), half(1, 0, 1), nm)
    pass_on(1)
    to_other(3, 0)
    to_other(1, 0)

    def relay(near):
        sender.arrive(("f+", near), both(near, 3), fm)
        sender.send(("f++", near), half(near, 3, 0), half(near, 3, 0), fp)
        to_other(near, 3)
        sender.arrive(("f-", near), both(near, 1), fp)
        sender.send(("f--", near), half(near, 1, 1), half(near, 1, 1), fm)
        to_other(near, 1)

    relay(0)
    sender.arrive("n++", half(2, 0, 0), nm)
    sender.arrive("n--", half(2, 0, 1), np_)
    pass_on(2)
    to_other(2, 0)
    for near in (3, 1, 2):
        relay(near)
    for near in (0, 3, 1, 2):
        sender.arrive(("f++", near), half(near, 2, 0), fm)
        sender.arrive(("f--", near), half(near, 2, 1), fp)
        to_other(near, 2)
    for near, far in core_order:
        at = buf.at[pl.ds(2 * place.other_at(near, far), 2)]
        sender.arrive(("core", near, far), at, other)


core_order = [(0, 0), (3, 0), (1, 0), (0, 3), (0, 1), (2, 0)]
core_order += [(n, f) for n in (3, 1, 2) for f in (3, 1)] + [(n, 2) for n in (0, 3, 1, 2)]


def reduce(place, sender, sums_hbm, own, core_in, far_half, far_full, near_half, near_full, load_sem):
    np_, nm, fp, fm, other = [{"pos": p} for p in place.partners()]
    order = [(near, far) for far in (2, 1, 3, 0) for near in (2, 1, 3, 0)]
    loads = {}
    for near, far in order:
        k = 4 * near + far
        sender.send(("core", near, far), sums_hbm.at[pl.ds(2 * place.other_at(near, far), 2)], core_in.at[near, far], other)
        loads[near, far] = pltpu.make_async_copy(
            sums_hbm.at[pl.ds(2 * place.at(near, far), 2)], own.at[near, far], load_sem.at[k]
        )
        loads[near, far].start()

    def pair(near, far):
        loads[near, far].wait()
        sender.arrive(("core", near, far), core_in.at[near, far], other)
        own[near, far] += core_in[near, far]

    for near in (2, 1, 3, 0):
        pair(near, 2)
        sender.send(("f++", near), own.at[near, 2, 0], far_half.at[near, 0], fp)
        sender.send(("f--", near), own.at[near, 2, 1], far_half.at[near, 1], fm)
    for near in (2, 1, 3, 0):
        pair(near, 1)
        sender.arrive(("f++", near), far_half.at[near, 0], fm)
        own[near, 1, 0] += far_half[near, 0]
        sender.send(("f+", near), own.at[near, 1], far_full.at[near, 0], fp)
        pair(near, 3)
        sender.arrive(("f--", near), far_half.at[near, 1], fp)
        own[near, 3, 1] += far_half[near, 1]
        sender.send(("f-", near), own.at[near, 3], far_full.at[near, 1], fm)

    def line(near):
        pair(near, 0)
        sender.arrive(("f+", near), far_full.at[near, 0], fm)
        sender.arrive(("f-", near), far_full.at[near, 1], fp)
        own[near, 0] += far_full[near, 0] + far_full[near, 1]

    line(2)
    sender.send("n++", own.at[2, 0, 0], near_half.at[0], np_)
    sender.send("n--", own.at[2, 0, 1], near_half.at[1], nm)
    line(1)
    sender.arrive("n++", near_half.at[0], nm)
    own[1, 0, 0] += near_half[0]
    sender.send("n+", own.at[1, 0], near_full.at[0], np_)
    line(3)
    sender.arrive("n--", near_half.at[1], np_)
    own[3, 0, 1] += near_half[1]
    sender.send("n-", own.at[3, 0], near_full.at[1], nm)
    line(0)
    sender.arrive("n+", near_full.at[0], nm)
    sender.arrive("n-", near_full.at[1], np_)
    own[0, 0] += near_full[0] + near_full[1]


def across(place, sender, mine, seen):
    tiles = seen.shape[0]
    seen[place.tile] = mine
    for k in range(1, tiles):
        to = (place.tile + k) % tiles
        sender.send(("tile", k), seen.at[place.tile], seen.at[place.tile], {"tile": to})
    for k in range(1, tiles):
        source = (place.tile + tiles - k) % tiles
        sender.arrive(("tile", k), seen.at[source], {"tile": source})
    total = seen[0]
    for k in range(1, tiles):
        total = total + seen[k]
    return total


def gather_kernel(object_ref, out_hbm, mine, send_sem, recv_sem, copy_sem):
    place = Place()
    for g in range(2):
        for p in range(2):
            for b in range(COLS):
                mine[g, COLS * p + b] = object_ref[p, 8 * g : 8 * g + 8, WIN * b : WIN * b + WIN]
    own = out_hbm.at[pl.ds(2 * place.at(0, 0), 2)]
    copy = pltpu.make_async_copy(mine, own, copy_sem)
    copy.start()
    greet(place, False)
    copy.wait()
    sender = Sender(send_sem, recv_sem)
    gather(place, sender, out_hbm)
    sender.finish()


def object_step(old, sums):
    for g in range(2):
        for b in range(COLS):
            scale = 1.0 / (sums[g, 2 * COLS + b] + 1.0)
            for p in range(2):
                yield g, p, b, (old[g, COLS * p + b] + sums[g, COLS * p + b]) * scale


def middle_kernel(
    sums_hbm, strip_hbm, out_hbm,
    old, own, core_in, far_half, far_full, near_half, near_full, seen, mine,
    load_sem, copy_sem, send_sem, recv_sem, send_sem2, recv_sem2,
):
    place = Place()
    here = pl.ds(2 * place.at(0, 0), 2)
    load = pltpu.make_async_copy(strip_hbm.at[here, pl.ds(0, 2 * COLS)], old, copy_sem)
    load.start()
    greet(place, True)
    first, second = Sender(send_sem, recv_sem), Sender(send_sem2, recv_sem2)
    reduce(place, first, sums_hbm, own, core_in, far_half, far_full, near_half, near_full, load_sem)
    total = own.at[0, 0]
    load.wait()
    for g, p, b, tile in object_step(old, total):
        mine[g, COLS * p + b] = tile
    mine[:, 2 * COLS] = across(place, first, total[:, 3 * COLS], seen)
    copy = pltpu.make_async_copy(mine, out_hbm.at[here], copy_sem)
    copy.start()
    copy.wait()
    gather(place, second, out_hbm)
    first.finish()
    second.finish()


def last_kernel(
    sums_hbm, strip_hbm, probe_ref, object_out, probe_out,
    old, own, core_in, far_half, far_full, near_half, near_full, seen, probe_sums,
    load_sem, copy_sem, send_sem, recv_sem, send_sem2, recv_sem2,
):
    place = Place()
    here = pl.ds(2 * place.at(0, 0), 2)
    load = pltpu.make_async_copy(strip_hbm.at[here, pl.ds(0, 2 * COLS)], old, copy_sem)
    load.start()
    greet(place, True)
    first, second = Sender(send_sem, recv_sem), Sender(send_sem2, recv_sem2)
    reduce(place, first, sums_hbm, own, core_in, far_half, far_full, near_half, near_full, load_sem)
    total = own.at[0, 0]
    probe_sums[here] = across(place, first, total[:, 3 * COLS], seen)
    load.wait()
    for g, p, b, tile in object_step(old, total):
        object_out[p, 8 * g : 8 * g + 8, WIN * b : WIN * b + WIN] = tile
    gather(place, second, probe_sums)
    stepped = probe_step(probe_ref, probe_sums.reshape(ROWS // WIN, WIN, WIN))
    for k in range(2):
        probe_out[k] = stepped[k]
    first.finish()
    second.finish()


GATHER_COPIES, REDUCE_COPIES = 36, 36


def dma(n):
    return pltpu.SemaphoreType.DMA((n,))


def reduce_scratch(tiles):
    chunk = (2, 3 * COLS + 1, 8, WIN)
    return [
        pltpu.VMEM((2, 2 * COLS, 8, WIN), f32),
        pltpu.VMEM((RING, RING) + chunk, f32),
        pltpu.VMEM((RING, RING) + chunk, f32),
        pltpu.VMEM((RING,) + chunk, f32),
        pltpu.VMEM((RING, 2) + chunk, f32),
        pltpu.VMEM(chunk, f32),
        pltpu.VMEM((2,) + chunk, f32),
        pltpu.VMEM((tiles, 2, 8, WIN), f32),
    ]


def params(collective_id):
    return pltpu.CompilerParams(
        collective_id=collective_id, has_side_effects=True, vmem_limit_bytes=40 * 1024 * 1024
    )


def gather_object(object_field):
    return pl.pallas_call(
        gather_kernel,
        out_shape=jax.ShapeDtypeStruct((GROUPS, 2 * COLS, 8, WIN), f32),
        in_specs=[VMEM],
        out_specs=ANY,
        scratch_shapes=[
            pltpu.VMEM((2, 2 * COLS, 8, WIN), f32), dma(GATHER_COPIES), dma(GATHER_COPIES), pltpu.SemaphoreType.DMA,
        ],
        compiler_params=params(0),
        name="gather_object",
    )(object_field)


def exchange_sems(tiles):
    copies = REDUCE_COPIES + tiles - 1
    return [
        dma(RING * RING), pltpu.SemaphoreType.DMA,
        dma(copies), dma(copies), dma(GATHER_COPIES), dma(GATHER_COPIES),
    ]


def middle(sums, strip):
    tiles = lax.axis_size("tile")
    return pl.pallas_call(
        middle_kernel,
        out_shape=jax.ShapeDtypeStruct((GROUPS, 2 * COLS + 1, 8, WIN), f32),
        in_specs=[ANY, ANY],
        out_specs=ANY,
        scratch_shapes=reduce_scratch(tiles) + [pltpu.VMEM((2, 2 * COLS + 1, 8, WIN), f32)] + exchange_sems(tiles),
        compiler_params=params(1),
        name="exchange_middle",
    )(sums, strip)


def last(sums, strip, probe, object_shape):
    tiles = lax.axis_size("tile")
    return pl.pallas_call(
        last_kernel,
        out_shape=(jax.ShapeDtypeStruct(object_shape, f32), jax.ShapeDtypeStruct(probe.shape, f32)),
        in_specs=[ANY, ANY, VMEM],
        out_specs=(VMEM, VMEM),
        scratch_shapes=reduce_scratch(tiles) + [pltpu.VMEM((GROUPS, 8, WIN), f32)] + exchange_sems(tiles),
        compiler_params=params(2),
        name="exchange_last",
    )(sums, strip, probe)


def per_device(object_field, illumination, row_offsets, col_offsets, counts, amplitudes):
    right, left = (jnp.asarray(table) for table in transform_tables())
    strip, probe = gather_object(object_field), illumination
    iterations = row_offsets.shape[0]
    for iteration in range(iterations):
        sums, probe = sweep(iteration, strip, probe, row_offsets, col_offsets, counts, amplitudes, right, left)
        if iteration + 1 < iterations:
            strip = middle(sums, strip)
    return last(sums, strip, probe, object_field.shape)


def solution(mesh):
    return jax.shard_map(
        per_device,
        mesh=mesh,
        in_specs=(
            P(None, "pos", "tile"),
            P(),
            P(None, ("tile", "pos")),
            P(None, ("tile", "pos")),
            P(None, ("tile", "pos")),
            P(None, ("tile", "pos"), None, None),
        ),
        out_specs=(P(None, "pos", "tile"), P()),
        check_vma=False,
    )
```

```python
import functools
import math

import jax
import jax.numpy as jnp
import ml_dtypes
import numpy as np
from jax import lax
from jax.experimental import pallas as pl
from jax.experimental.pallas import tpu as pltpu
from jax.sharding import PartitionSpec as P

WIN = 128
ROWS = 512
GROUPS = ROWS // 8
COLS = ROWS // WIN
OTILES, STILES = 2 * COLS, 3 * COLS
BLOCK = 8
RING = 4
AWAY, ALL = (2, 1, 3), (2, 1, 3, 0)
MESH = pl.DeviceIdType.MESH
f32 = jnp.float32


def transform_tables():
    ramp = np.arange(WIN)
    angle = -2.0 * np.pi / WIN * (np.outer(ramp, ramp) % WIN)
    c, s = np.cos(angle) / math.sqrt(WIN), np.sin(angle) / math.sqrt(WIN)
    return np.stack([np.block([[c, s], [-s, c]]), np.block([[c, -s], [s, c]])]).astype(np.float32)


def split(x):
    high = x.astype(jnp.bfloat16)
    return high, (x - high.astype(f32)).astype(jnp.bfloat16)


def blocks(rows):
    halves = [[split(part) for part in row] for row in rows]
    return [jnp.concatenate([jnp.concatenate([part[k] for part in row], 1) for row in halves], 0) for k in range(2)]


def dot(a, b):
    return jnp.dot(a, b, preferred_element_type=f32)


def along_columns(pairs, table):
    high, low = blocks(pairs)
    both = dot(jnp.concatenate([high, low], 0), table[: 2 * WIN])
    return both[: 2 * WIN] + both[2 * WIN :] + dot(high, table[2 * WIN :])


def along_rows(y, table):
    quarter = [[y[j * WIN : (j + 1) * WIN, p * WIN : (p + 1) * WIN] for j in range(2)] for p in range(2)]
    high, low = blocks(quarter)
    both = dot(table, high)
    z = both[: 2 * WIN] + both[2 * WIN :] + dot(table[: 2 * WIN], low)
    return [(z[:WIN, j * WIN : (j + 1) * WIN], z[WIN:, j * WIN : (j + 1) * WIN]) for j in range(2)]


def probe_step(probe, sums):
    scale = lax.rsqrt(sums[2] + 1.0)
    return [probe[k] + (sums[k] - probe[k] * sums[2]) * scale for k in range(2)]


def sweep_kernel(
    iteration, updates,
    rows_hbm, cols_hbm, counts_hbm, rows_in, cols_in, counts_in, probe_hbm, old_hbm, tables_hbm, strip_hbm,
    amp_hbm, amp_in, out_hbm, sums_out, probe_out,
    rows, cols, counts, rows2, cols2, counts2, tables, split_tables, probe, old_sums, strip, sums, amp, probe_sums,
    small_sem, strip_sem, amp_sem, out_sem,
):
    half = amp.shape[0] // 2
    core = lax.axis_index("pos") % 2
    small = [
        (counts_hbm, counts), (counts_in, counts2), (rows_hbm, rows), (rows_in, rows2), (cols_hbm, cols),
        (cols_in, cols2), (probe_hbm, probe), (tables_hbm, tables),
    ]
    if updates:
        small.append((old_hbm, old_sums))
    copies = [pltpu.make_async_copy(src, dst, small_sem.at[k]) for k, (src, dst) in enumerate(small)]
    copies += [pltpu.make_async_copy(strip_hbm.at[:, k], strip.at[k], strip_sem.at[k]) for k in range(OTILES)]
    for copy in copies:
        copy.start()
    sums_rows = sums.reshape(STILES, ROWS, WIN)
    strip_rows = strip.reshape(OTILES, ROWS, WIN)
    probe_rows = probe_sums.reshape(ROWS // WIN, WIN, WIN)
    for k in range(STILES):
        sums_rows[k] = jnp.zeros((ROWS, WIN), f32)
    for k in range(ROWS // WIN):
        probe_rows[k] = jnp.zeros((WIN, WIN), f32)
    for copy in copies[:2]:
        copy.wait()
    mine = (counts[0, iteration] + 1 - core) // 2
    count = mine + (counts2[0, iteration] + 1 - core) // 2
    amp_copies = []
    for source, live in ((0, mine), (1, count - mine)):
        for k in range(half // GRAIN):
            part, at = pl.ds(k * GRAIN, GRAIN), pl.ds(source * half + k * GRAIN, GRAIN)
            src = amp_in.at[iteration, part] if source else amp_hbm.at[iteration, part, core]
            copy = pltpu.make_async_copy(src, amp.at[at], amp_sem.at[source, k])
            amp_copies.append((live > k * GRAIN, copy))
    for needed, copy in amp_copies:
        pl.when(needed)(copy.start)
    for copy in copies[2:]:
        copy.wait()
    if updates:
        stepped = probe_step(probe, old_sums.reshape(ROWS // WIN, WIN, WIN))
        for k in range(2):
            probe[k] = stepped[k]
    probe_out[...] = probe[...]
    for k in range(2):
        split_tables[k, : 2 * WIN], split_tables[k, 2 * WIN :] = split(tables[k])
    for needed, copy in amp_copies:
        pl.when(needed)(copy.wait)
    lane = lax.broadcasted_iota(jnp.int32, (WIN, WIN), 1)

    def body(k, carry):
        def find(number):
            theirs = number >= mine
            place = jnp.minimum(jnp.where(theirs, number - mine, number), half - 1)
            slot = 2 * place + core
            row = jnp.where(theirs, rows2[iteration, slot], rows[iteration, slot])
            col = jnp.where(theirs, cols2[iteration, slot], cols[iteration, slot])
            first, turn = col // WIN, col % WIN
            second = jnp.minimum(first + 1, COLS - 1)
            return number, jnp.where(theirs, half + place, place), pl.ds(row, WIN), first, second, turn

        def window(found):
            _, _, row, first, second, turn = found
            here = lane >= turn
            q = [
                jnp.where(here, strip_rows[COLS * p + first, row, :], strip_rows[COLS * p + second, row, :])
                for p in range(2)
            ]
            return here, q, [pltpu.roll(probe[p], turn, 1) for p in range(2)]

        def exit_wave(found):
            _, (qr, qi), (pr, pi) = window(found)
            return pr * qr - pi * qi, pr * qi + pi * qr

        def scaled(found, z):
            number, place = found[:2]
            re, im = z
            factor = amp[place] * lax.rsqrt(re * re + im * im + 1.0)
            factor = jnp.where(number < count, factor, 0.0)
            return re * factor, im * factor

        def add(found, g):
            number, _, row, first, second, turn = found
            here, (qr, qi), (pr, pi) = window(found)
            gr, gi = g
            live = (number < count).astype(f32)
            for p, term in enumerate((pr * gr + pi * gi, pr * gi - pi * gr, (pr * pr + pi * pi) * live)):
                sums_rows[COLS * p + first, row, :] += jnp.where(here, term, 0.0)
                sums_rows[COLS * p + second, row, :] += jnp.where(here, 0.0, term)
            back = jnp.where(turn == 0, 0, WIN - turn)
            for p, term in enumerate((qr * gr + qi * gi, qr * gi - qi * gr, (qr * qr + qi * qi) * live)):
                probe_rows[p] += pltpu.roll(term, back, 1)

        pairs = BLOCK // 2
        found, value = [None] * pairs, [None] * pairs
        for step in range(pairs + 6):
            for stage in range(7):
                pair = step - stage
                if not 0 <= pair < pairs:
                    continue
                if stage == 0:
                    found[pair] = [find(k * BLOCK + 2 * pair + j) for j in range(2)]
                    value[pair] = [exit_wave(slot) for slot in found[pair]]
                elif stage in (1, 4):
                    value[pair] = along_columns(value[pair], split_tables[stage // 4])
                elif stage in (2, 5):
                    value[pair] = along_rows(value[pair], split_tables[1 - stage // 4])
                elif stage == 3:
                    value[pair] = [scaled(slot, z) for slot, z in zip(found[pair], value[pair])]
                else:
                    for slot, g in zip(found[pair], value[pair]):
                        add(slot, g)
        return carry

    lax.fori_loop(0, (count + BLOCK - 1) // BLOCK, body, 0)
    outs = [pltpu.make_async_copy(sums.at[k], out_hbm.at[:, k], out_sem.at[k]) for k in range(STILES)]
    outs.append(pltpu.make_async_copy(probe_sums, sums_out, out_sem.at[STILES]))
    for copy in outs:
        copy.start()
    for copy in outs:
        copy.wait()


GRAIN = 4
VMEM_BYTES = 60 * 1024 * 1024
ANY = pl.BlockSpec(memory_space=pl.ANY)
VMEM = pl.BlockSpec(memory_space=pltpu.VMEM)


def dma(*shape):
    return pltpu.SemaphoreType.DMA(shape)


def sweep(iteration, strip, probe, old_sums, offsets, amplitudes, amplitudes_in, tables):
    cap = offsets[0].shape[1]
    updates = old_sums is not None
    return pl.pallas_call(
        functools.partial(sweep_kernel, iteration, updates),
        out_shape=(
            jax.ShapeDtypeStruct((GROUPS, STILES, 8, WIN), f32),
            jax.ShapeDtypeStruct((GROUPS, 8, WIN), f32),
            jax.ShapeDtypeStruct(probe.shape, f32),
        ),
        in_specs=[ANY] * 12,
        out_specs=(ANY, ANY, VMEM),
        scratch_shapes=[pltpu.SMEM(array.shape, jnp.int32) for array in offsets]
        + [
            pltpu.VMEM(tables.shape, f32),
            pltpu.VMEM((2, 4 * WIN, 2 * WIN), jnp.bfloat16),
            pltpu.VMEM(probe.shape, f32),
            pltpu.VMEM((GROUPS, 8, WIN), f32),
            pltpu.VMEM((OTILES, GROUPS, 8, WIN), f32),
            pltpu.VMEM((STILES, GROUPS, 8, WIN), f32),
            pltpu.VMEM((cap, WIN, WIN), f32),
            pltpu.VMEM((GROUPS, 8, WIN), f32),
            dma(10),
            dma(OTILES),
            dma(2, cap // 2 // GRAIN),
            dma(STILES + 1),
        ],
        compiler_params=pltpu.CompilerParams(vmem_limit_bytes=VMEM_BYTES),
        name="sweep",
    )(*offsets, probe, old_sums if updates else probe, tables, strip, amplitudes, amplitudes_in)


class Place:
    def __init__(self):
        pos = lax.axis_index("pos")
        self.tile = lax.axis_index("tile")
        core, y, x = pos % 2, pos // 2 % RING, pos // (2 * RING)
        self.core = core
        self.near, self.far = x + core * (y - x), y + core * (x - y)
        self.near_step, self.far_step = 8 - 6 * core, 2 + 6 * core

    def at(self, near, far):
        return (self.near + near) % RING * self.near_step + (self.far + far) % RING * self.far_step + self.core

    def other_at(self, near, far):
        return (self.far + near) % RING * self.far_step + (self.near + far) % RING * self.near_step + 1 - self.core

    def near_peer(self, k):
        return {"pos": self.at(k, 0)}

    def far_peer(self, k):
        return {"pos": self.at(0, k)}

    def other(self):
        return {"pos": self.other_at(0, 0)}

    def tile_peer(self, k, tiles):
        return {"tile": (self.tile + k) % tiles}


def greet(place, tiles):
    barrier = pltpu.get_barrier_semaphore()
    peers = [place.other()] + [place.near_peer(k) for k in AWAY] + [place.far_peer(k) for k in AWAY]
    peers += [place.tile_peer(k, tiles) for k in range(1, tiles)]
    for peer in peers:
        pl.semaphore_signal(barrier, inc=1, device_id=peer, device_id_type=MESH)
    pl.semaphore_wait(barrier, len(peers))


class Sender:
    def __init__(self, send_sem, recv_sem):
        self.send_sem, self.recv_sem = send_sem, recv_sem
        self.names, self.sent = {}, []

    def copy(self, name, src, dst, device):
        k = self.names.setdefault(name, len(self.names))
        return pltpu.make_async_remote_copy(
            src_ref=src, dst_ref=dst, send_sem=self.send_sem.at[k], recv_sem=self.recv_sem.at[k],
            device_id=device, device_id_type=MESH)

    def send(self, name, src, dst, device):
        copy = self.copy(name, src, dst, device)
        copy.start()
        self.sent.append(copy)

    def arrive(self, name, dst, device):
        self.copy(name, dst, dst, device).wait_recv()

    def finish(self):
        for copy in self.sent:
            copy.wait_send()


class Reduce:
    def __init__(self, place, sender, src, own, core_in, far_in, near_in, load_sem, relay=False):
        self.place, self.sender, self.src, self.own = place, sender, src, own
        self.core_in, self.far_in, self.near_in, self.load_sem = core_in, far_in, near_in, load_sem
        self.loads = {}

    def load(self):
        for far in ALL:
            for near in ALL:
                copy = pltpu.make_async_copy(
                    self.src.at[pl.ds(2 * self.place.at(near, far), 2)], self.own.at[:, near, far],
                    self.load_sem.at[4 * near + far])
                copy.start()
                self.loads[near, far] = copy

    def core_send(self, h):
        for far in ALL:
            for near in ALL:
                self.sender.send(("core", h, near, far), self.src.at[2 * self.place.other_at(near, far) + h],
                                 self.core_in.at[h, near, far], self.place.other())

    def pair(self, h, near, far):
        copy = self.loads.pop((near, far), None)
        if copy is not None:
            copy.wait()
        self.sender.arrive(("core", h, near, far), self.core_in.at[h, near, far], self.place.other())
        self.own[h, near, far] += self.core_in[h, near, far]

    def far_send(self, h, fars=AWAY):
        for far in fars:
            for near in ALL:
                self.pair(h, near, far)
                self.sender.send(("far", h, near, far), self.own.at[h, near, far], self.far_in.at[h, far - 1, near],
                                 self.place.far_peer(far))

    relay_in = None

    def far_first(self, h):
        for near in ALL:
            self.pair(h, near, 2)
            for k, far in enumerate((1, 3)):
                part = pl.ds(k * STILES // 2, STILES // 2)
                self.sender.send(("relay", h, near, far), self.own.at[h, near, 2, part], self.relay_in.at[h, k, near],
                                 self.place.far_peer(far))

    def far_second(self, h):
        for near in ALL:
            for k, far in enumerate((1, 3)):
                self.pair(h, near, far)
                part = pl.ds(k * STILES // 2, STILES // 2)
                at = self.relay_in.at[h, k, near]
                self.sender.arrive(("relay", h, near, far), at, self.place.far_peer(RING - far))
                self.own[h, near, far, part] += at[...]
                self.sender.send(("far", h, near, far), self.own.at[h, near, far], self.far_in.at[h, far - 1, near],
                                 self.place.far_peer(far))

    def line(self, h, near):
        self.pair(h, near, 0)
        total = self.own[h, near, 0]
        for far in (1, 3) if self.relay_in is not None else (1, 3, 2):
            at = self.far_in.at[h, far - 1, near]
            self.sender.arrive(("far", h, near, far), at, self.place.far_peer(RING - far))
            total = total + at[...]
        self.own[h, near, 0] = total

    def near_send(self, h):
        for near in AWAY:
            self.line(h, near)
            self.sender.send(("near", h, near), self.own.at[h, near, 0], self.near_in.at[h, near - 1],
                             self.place.near_peer(near))

    def total(self, h):
        self.line(h, 0)
        total = self.own[h, 0, 0]
        for near in (1, 3, 2):
            at = self.near_in.at[h, near - 1]
            self.sender.arrive(("near", h, near), at, self.place.near_peer(RING - near))
            total = total + at[...]
        return total


class Gather:
    def __init__(self, place, sender, buf, name="o"):
        self.place, self.sender, self.buf, self.name = place, sender, buf, name

    def at(self, h, near, far):
        return self.buf.at[2 * self.place.at(near, far) + h]

    def spread(self, h, near):
        for far in (1, 3) if near in self.relays else AWAY:
            self.sender.send((self.name, "far", h, near, far), self.at(h, near, 0), self.at(h, near, 0), self.place.far_peer(far))

    def to_core(self, h, near, far):
        self.sender.send((self.name, "core", h, near, far), self.at(h, near, far), self.at(h, near, far), self.place.other())

    def start(self, h):
        for near in AWAY:
            self.sender.send((self.name, "near", h, near), self.at(h, 0, 0), self.at(h, 0, 0), self.place.near_peer(near))
        self.spread(h, 0)
        self.to_core(h, 0, 0)

    relays = ()

    def half(self, h, near, far, k):
        return self.buf.at[2 * self.place.at(near, far) + h, pl.ds(4 * k, 4)]

    def relay(self, h, near):
        for k, far in enumerate((1, 3)):
            back = RING - far
            self.sender.arrive((self.name, "far", h, near, far), self.at(h, near, back), self.place.far_peer(back))
            at = self.half(h, near, back, k)
            self.sender.send((self.name, "relay", h, near, far), at, at, self.place.far_peer(far))
            self.to_core(h, near, back)

    def relayed(self, h, near):
        for k, far in enumerate((1, 3)):
            self.sender.arrive((self.name, "relay", h, near, far), self.half(h, near, 2, k), self.place.far_peer(RING - far))
        self.to_core(h, near, 2)

    def middle(self, h):
        for near in (1, 3, 2):
            self.sender.arrive((self.name, "near", h, RING - near), self.at(h, near, 0), self.place.near_peer(near))
            self.spread(h, near)
        for near in (1, 3, 2):
            self.to_core(h, near, 0)

    def end(self, h, nears=(0, 1, 3, 2)):
        for near in self.relays:
            self.relay(h, near)
        for near in nears:
            if near in self.relays:
                continue
            for far in (1, 3, 2):
                self.sender.arrive((self.name, "far", h, near, RING - far), self.at(h, near, far), self.place.far_peer(far))
                self.to_core(h, near, far)

    def done(self, h):
        for near in self.relays:
            self.relayed(h, near)
        for near in range(RING):
            for far in range(RING):
                at = self.buf.at[2 * self.place.other_at(near, far) + h]
                self.sender.arrive((self.name, "core", h, near, far), at, self.place.other())


class ProbeSum:
    def __init__(self, place, sender, src, tiles, own, core_in, table, far_in, line, near_in, seen, all_, other_all, load_sem):
        self.place, self.sender, self.src, self.tiles = place, sender, src, tiles
        self.own, self.core_in, self.table, self.far_in, self.line = own, core_in, table, far_in, line
        self.near_in, self.seen, self.all, self.other_all, self.load_sem = near_in, seen, all_, other_all, load_sem

    def load(self):
        self.copy = pltpu.make_async_copy(self.src.at[:, :, self.place.core], self.own, self.load_sem)
        self.copy.start()

    def core(self):
        self.sender.send("pcore", self.src.at[:, :, 1 - self.place.core], self.core_in, self.place.other())

    def far(self):
        place = self.place
        self.copy.wait()
        self.sender.arrive("pcore", self.core_in, place.other())
        for x in range(RING):
            for y in range(RING):
                near, far = x + place.core * (y - x), y + place.core * (x - y)
                self.table[near, far] = self.own[x, y] + self.core_in[x, y]
        for k in AWAY:
            src = self.table.at[:, (place.far + k) % RING]
            self.sender.send(("pfar", k), src, self.far_in.at[k - 1], place.far_peer(k))

    def near(self):
        place = self.place
        total = self.table[:, place.far]
        for k in (1, 3, 2):
            self.sender.arrive(("pfar", k), self.far_in.at[k - 1], place.far_peer(RING - k))
            total = total + self.far_in[k - 1]
        self.line[...] = total
        for k in AWAY:
            src = self.line.at[(place.near + k) % RING]
            self.sender.send(("pnear", k), src, self.near_in.at[k - 1], place.near_peer(k))

    def across(self):
        place = self.place
        total = self.line[place.near]
        for k in (1, 3, 2):
            self.sender.arrive(("pnear", k), self.near_in.at[k - 1], place.near_peer(RING - k))
            total = total + self.near_in[k - 1]
        self.seen[place.tile] = total
        for k in range(1, self.tiles):
            at = self.seen.at[place.tile]
            self.sender.send(("ptile", k), at, at, place.tile_peer(k, self.tiles))

    def back_near(self):
        place = self.place
        for k in range(1, self.tiles):
            source = (place.tile + self.tiles - k) % self.tiles
            self.sender.arrive(("ptile", k), self.seen.at[source], {"tile": source})
        total = self.seen[0]
        for k in range(1, self.tiles):
            total = total + self.seen[k]
        self.all[place.near, place.far] = total
        at = self.all.at[place.near, place.far]
        for k in AWAY:
            self.sender.send(("pback", k), at, at, place.near_peer(k))

    def back_far(self):
        place = self.place
        for k in (1, 3, 2):
            at = self.all.at[(place.near + RING - k) % RING, place.far]
            self.sender.arrive(("pback", k), at, place.near_peer(RING - k))
        at = self.all.at[:, place.far]
        for k in AWAY:
            self.sender.send(("pout", k), at, at, place.far_peer(k))

    def back_core(self):
        place = self.place
        for k in (1, 3, 2):
            at = self.all.at[:, (place.far + RING - k) % RING]
            self.sender.arrive(("pout", k), at, place.far_peer(RING - k))
        self.sender.send("pother", self.all, self.other_all, place.other())

    def finish(self, out):
        core = self.place.core
        self.sender.arrive("pother", self.other_all, self.place.other())
        for near in range(RING):
            for far in range(RING):
                x, y = near + core * (far - near), far + core * (near - far)
                out[x, y, core] = self.all[near, far]
                out[y, x, 1 - core] = self.other_all[near, far]


def gather_kernel(
    object_ref, amp_hbm, rows_hbm, cols_hbm, counts_hbm, out_hbm, amp_in, rows_in, cols_in, counts_in,
    mine, send_sem, recv_sem, copy_sem,
):
    place = Place()
    for g in range(2):
        for p in range(2):
            for b in range(COLS):
                mine[g, COLS * p + b] = object_ref[p, 8 * g : 8 * g + 8, WIN * b : WIN * b + WIN]
    copy = pltpu.make_async_copy(mine, out_hbm.at[pl.ds(2 * place.at(0, 0), 2)], copy_sem)
    copy.start()
    greet(place, 1)
    copy.wait()
    sender = Sender(send_sem, recv_sem)
    strip = Gather(place, sender, out_hbm)
    strip.start(0)
    strip.start(1)
    other = place.other()
    moves = [(counts_hbm, counts_in), (rows_hbm, rows_in), (cols_hbm, cols_in)]
    moves += [(amp_hbm.at[k, :, 1 - place.core], amp_in.at[k]) for k in range(amp_in.shape[0])]
    for k, (src, dst) in enumerate(moves):
        sender.send(("move", k), src, dst, other)
    for h in range(2):
        strip.middle(h)
    for h in range(2):
        strip.end(h)
    for h in range(2):
        strip.done(h)
    for k, (_, dst) in enumerate(moves):
        sender.arrive(("move", k), dst, other)
    sender.finish()


def exchange_kernel(
    tiles, last, sums_hbm, probe_src, strip_hbm, *refs,
):
    if last:
        probe_ref, object_out, probe_out = refs[:3]
        refs = refs[3:]
    else:
        out_hbm, sums_out = refs[:2]
        refs = refs[2:]
    (old, own, core_in, far_in, near_in, relay_in, mine,
     p_own, p_core, p_table, p_far, p_line, p_near, p_seen, p_all, p_other, p_out,
     load_sem, copy_sem, send_sem, recv_sem, send_sem2, recv_sem2, send_sem3, recv_sem3) = refs
    place = Place()
    here = pl.ds(2 * place.at(0, 0), 2)
    load = pltpu.make_async_copy(strip_hbm.at[here], old, copy_sem.at[0])
    load.start()
    first, second, third = Sender(send_sem, recv_sem), Sender(send_sem2, recv_sem2), Sender(send_sem3, recv_sem3)
    sums = Reduce(place, first, sums_hbm, own, core_in, far_in, near_in, load_sem)
    sums.relay_in = relay_in
    probe = ProbeSum(
        place, third, probe_src, tiles, p_own, p_core, p_table, p_far, p_line, p_near, p_seen, p_all, p_other,
        copy_sem.at[3],
    )
    probe.load()
    sums.load()
    greet(place, tiles)
    probe.core()
    sums.core_send(0)
    sums.core_send(1)
    probe.far()
    sums.far_first(0)
    sums.far_first(1)
    probe.near()
    sums.far_second(0)
    probe.across()
    sums.far_second(1)
    sums.near_send(0)
    probe.back_near()
    sums.near_send(1)
    strip = None if last else Gather(place, second, out_hbm)

    def step(h):
        total = sums.total(h)
        if h == 0:
            load.wait()
        for b in range(COLS):
            scale = 1.0 / (total[2 * COLS + b] + 1.0)
            for p in range(2):
                tile = (old[h, COLS * p + b] + total[COLS * p + b]) * scale
                if last:
                    object_out[p, 8 * h : 8 * h + 8, WIN * b : WIN * b + WIN] = tile
                else:
                    mine[h, COLS * p + b] = tile
        if not last:
            copy = pltpu.make_async_copy(mine.at[h], strip.at(h, 0, 0), copy_sem.at[1 + h])
            copy.start()
            copy.wait()
            strip.start(h)

    probe.back_far()
    step(0)
    step(1)
    probe.back_core()
    if last:
        probe.finish(p_out)
        stepped = probe_step(probe_ref, p_out.reshape(ROWS // WIN, WIN, WIN))
        for k in range(2):
            probe_out[k] = stepped[k]
    else:
        for h in range(2):
            strip.middle(h)
        probe.finish(sums_out)
        for h in range(2):
            strip.end(h)
        for h in range(2):
            strip.done(h)
    for sender in (first, second, third):
        sender.finish()


def params(collective_id):
    return pltpu.CompilerParams(collective_id=collective_id, has_side_effects=True, vmem_limit_bytes=VMEM_BYTES)


GATHER_COPIES, REDUCE_COPIES = 62, 70


def gather_object(object_field, amplitudes, offsets):
    copies = GATHER_COPIES + 3 + amplitudes.shape[0]
    halves = amplitudes.shape[:2] + amplitudes.shape[3:]
    return pl.pallas_call(
        gather_kernel,
        out_shape=[jax.ShapeDtypeStruct((GROUPS, OTILES, 8, WIN), f32), jax.ShapeDtypeStruct(halves, f32)]
        + [jax.ShapeDtypeStruct(array.shape, jnp.int32) for array in offsets],
        in_specs=[VMEM] + [ANY] * 4,
        out_specs=[ANY] * 5,
        scratch_shapes=[pltpu.VMEM((2, OTILES, 8, WIN), f32), dma(copies), dma(copies), pltpu.SemaphoreType.DMA],
        compiler_params=params(0),
        name="gather_object",
    )(object_field, amplitudes, *offsets)


def exchange(sums, probe_sums, strip, probe, object_shape):
    tiles = lax.axis_size("tile")
    is_last = probe is not None
    by_device = (RING, RING, 2, 2, 8, WIN)
    if is_last:
        out_shape = (jax.ShapeDtypeStruct(object_shape, f32), jax.ShapeDtypeStruct(probe.shape, f32))
        out_specs = (VMEM, VMEM)
    else:
        out_shape = (jax.ShapeDtypeStruct(strip.shape, f32), jax.ShapeDtypeStruct(by_device, f32))
        out_specs = (ANY, VMEM)
    group, pair = (STILES, 8, WIN), (2, 8, WIN)
    buffers = [
        (2, OTILES, 8, WIN), (2, RING, RING) + group, (2, RING, RING) + group, (2, 3, RING) + group, (2, 3) + group,
        (2, 2, RING, STILES // 2, 8, WIN), (2, OTILES, 8, WIN),
        (RING, RING) + pair, (RING, RING) + pair, (RING, RING) + pair, (3, RING) + pair, (RING,) + pair, (3,) + pair,
        (tiles,) + pair, (RING, RING) + pair, (RING, RING) + pair, by_device,
    ]
    return pl.pallas_call(
        functools.partial(exchange_kernel, tiles, is_last),
        out_shape=out_shape,
        in_specs=[ANY, ANY, ANY] + ([VMEM] if is_last else []),
        out_specs=out_specs,
        scratch_shapes=[pltpu.VMEM(shape, f32) for shape in buffers]
        + [dma(RING * RING), dma(4)]
        + [dma(REDUCE_COPIES)] * 2 + [dma(GATHER_COPIES)] * 2 + [dma(14 + tiles - 1)] * 2,
        compiler_params=params(2 if is_last else 1),
        name="exchange_last" if is_last else "exchange_middle",
    )(sums, probe_sums.reshape(by_device), strip, *([probe] if is_last else []))


def per_device(object_field, illumination, row_offsets, col_offsets, counts, amplitudes):
    tables = jnp.asarray(transform_tables())
    offsets = [row_offsets, col_offsets, counts.T]
    iterations, cap = row_offsets.shape
    amplitudes = amplitudes.reshape(iterations, cap // 2, 2, WIN, WIN)
    strip, amplitudes_in, *offsets_in = gather_object(object_field, amplitudes, offsets)
    probe, old_sums = illumination, None
    for iteration in range(iterations):
        sums, probe_sums, probe = sweep(
            iteration, strip, probe, old_sums, offsets + offsets_in, amplitudes, amplitudes_in, tables
        )
        if iteration + 1 < iterations:
            strip, old_sums = exchange(sums, probe_sums, strip, None, None)
            old_sums = old_sums.reshape(GROUPS, 8, WIN)
    return exchange(sums, probe_sums, strip, probe, object_field.shape)


def solution(mesh):
    return jax.shard_map(
        per_device,
        mesh=mesh,
        in_specs=(
            P(None, "pos", "tile"),
            P(),
            P(None, ("tile", "pos")),
            P(None, ("tile", "pos")),
            P(None, ("tile", "pos")),
            P(None, ("tile", "pos"), None, None),
        ),
        out_specs=(P(None, "pos", "tile"), P()),
        check_vma=False,
    )
```

```python
import functools
import math

import jax
import jax.numpy as jnp
import ml_dtypes
import numpy as np
from jax import lax
from jax.experimental import pallas as pl
from jax.experimental.pallas import tpu as pltpu
from jax.sharding import PartitionSpec as P

WIN = 128
ROWS = 512
GROUPS = ROWS // 8
COLS = ROWS // WIN
PTILES = 3 * WIN // 8
OTILES, STILES = 2 * COLS, 3 * COLS
BLOCK = 8
RING = 4
AWAY, ALL = (2, 1, 3), (2, 1, 3, 0)
MESH = pl.DeviceIdType.MESH
f32 = jnp.float32


def transform_tables():
    ramp = np.arange(WIN)
    angle = -2.0 * np.pi / WIN * (np.outer(ramp, ramp) % WIN)
    c, s = np.cos(angle) / math.sqrt(WIN), np.sin(angle) / math.sqrt(WIN)
    return np.stack([np.block([[c, s], [-s, c]]), np.block([[c, -s], [s, c]])]).astype(np.float32)


def split(x):
    high = x.astype(jnp.bfloat16)
    return high, (x - high.astype(f32)).astype(jnp.bfloat16)


def blocks(rows):
    halves = [[split(part) for part in row] for row in rows]
    return [jnp.concatenate([jnp.concatenate([part[k] for part in row], 1) for row in halves], 0) for k in range(2)]


def dot(a, b):
    return jnp.dot(a, b, preferred_element_type=f32)


def along_columns(pairs, table):
    high, low = blocks(pairs)
    both = dot(jnp.concatenate([high, low], 0), table[: 2 * WIN])
    return both[: 2 * WIN] + both[2 * WIN :] + dot(high, table[2 * WIN :])


def along_rows(y, table):
    quarter = [[y[j * WIN : (j + 1) * WIN, p * WIN : (p + 1) * WIN] for j in range(2)] for p in range(2)]
    high, low = blocks(quarter)
    both = dot(table, high)
    z = both[: 2 * WIN] + both[2 * WIN :] + dot(table[: 2 * WIN], low)
    return [(z[:WIN, j * WIN : (j + 1) * WIN], z[WIN:, j * WIN : (j + 1) * WIN]) for j in range(2)]


def probe_step(probe, sums):
    scale = lax.rsqrt(sums[2] + 1.0)
    return [probe[k] + (sums[k] - probe[k] * sums[2]) * scale for k in range(2)]


def sweep_kernel(
    iteration, updates,
    rows_hbm, cols_hbm, counts_hbm, rows_in, cols_in, counts_in, probe_hbm, old_hbm, tables_hbm, strip_hbm,
    amp_hbm, amp_in, out_hbm, sums_out, probe_out,
    rows, cols, counts, rows2, cols2, counts2, tables, split_tables, probe, old_sums, strip, sums, amp, probe_sums,
    small_sem, strip_sem, amp_sem, out_sem,
):
    half = amp.shape[0] // 2
    core = lax.axis_index("pos") % 2
    small = [
        (counts_hbm, counts), (counts_in, counts2), (rows_hbm, rows), (rows_in, rows2), (cols_hbm, cols),
        (cols_in, cols2), (probe_hbm, probe), (tables_hbm, tables),
    ]
    if updates:
        small.append((old_hbm, old_sums))
    copies = [pltpu.make_async_copy(src, dst, small_sem.at[k]) for k, (src, dst) in enumerate(small)]
    copies += [pltpu.make_async_copy(strip_hbm.at[:, k], strip.at[k], strip_sem.at[k]) for k in range(OTILES)]
    for copy in copies:
        copy.start()
    sums_rows = sums.reshape(STILES, ROWS, WIN)
    strip_rows = strip.reshape(OTILES, ROWS, WIN)
    probe_rows = probe_sums.reshape(3, WIN, WIN)
    for k in range(STILES):
        sums_rows[k] = jnp.zeros((ROWS, WIN), f32)
    for k in range(3):
        probe_rows[k] = jnp.zeros((WIN, WIN), f32)
    for copy in copies[:2]:
        copy.wait()
    mine = (counts[0, iteration] + 1 - core) // 2
    count = mine + (counts2[0, iteration] + 1 - core) // 2
    amp_copies = []
    for source, live in ((0, mine), (1, count - mine)):
        for k in range(half // GRAIN):
            part, at = pl.ds(k * GRAIN, GRAIN), pl.ds(source * half + k * GRAIN, GRAIN)
            src = amp_in.at[iteration, part] if source else amp_hbm.at[iteration, part, core]
            copy = pltpu.make_async_copy(src, amp.at[at], amp_sem.at[source, k])
            amp_copies.append((live > k * GRAIN, copy))
    for needed, copy in amp_copies:
        pl.when(needed)(copy.start)
    for copy in copies[2:]:
        copy.wait()
    if updates:
        stepped = probe_step(probe, old_sums.reshape(3, WIN, WIN))
        for k in range(2):
            probe[k] = stepped[k]
    probe_out[...] = probe[...]
    for k in range(2):
        split_tables[k, : 2 * WIN], split_tables[k, 2 * WIN :] = split(tables[k])
    for needed, copy in amp_copies:
        pl.when(needed)(copy.wait)
    lane = lax.broadcasted_iota(jnp.int32, (WIN, WIN), 1)

    def work(begin, size):
        def find(number):
            theirs = number >= mine
            place = jnp.minimum(jnp.where(theirs, number - mine, number), half - 1)
            slot = 2 * place + core
            row = jnp.where(theirs, rows2[iteration, slot], rows[iteration, slot])
            col = jnp.where(theirs, cols2[iteration, slot], cols[iteration, slot])
            first, turn = col // WIN, col % WIN
            second = jnp.minimum(first + 1, COLS - 1)
            return number, jnp.where(theirs, half + place, place), pl.ds(row, WIN), first, second, turn

        def window(found):
            _, _, row, first, second, turn = found
            here = lane >= turn
            q = [
                jnp.where(here, strip_rows[COLS * p + first, row, :], strip_rows[COLS * p + second, row, :])
                for p in range(2)
            ]
            return here, q, [pltpu.roll(probe[p], turn, 1) for p in range(2)]

        def exit_wave(found):
            _, (qr, qi), (pr, pi) = window(found)
            return pr * qr - pi * qi, pr * qi + pi * qr

        def scaled(found, z):
            number, place = found[:2]
            re, im = z
            factor = amp[place] * lax.rsqrt(re * re + im * im + 1.0)
            factor = jnp.where(number < count, factor, 0.0)
            return re * factor, im * factor

        def add(found, g):
            number, _, row, first, second, turn = found
            here, (qr, qi), (pr, pi) = window(found)
            gr, gi = g
            live = (number < count).astype(f32)
            for p, term in enumerate((pr * gr + pi * gi, pr * gi - pi * gr, (pr * pr + pi * pi) * live)):
                sums_rows[COLS * p + first, row, :] += jnp.where(here, term, 0.0)
                sums_rows[COLS * p + second, row, :] += jnp.where(here, 0.0, term)
            back = jnp.where(turn == 0, 0, WIN - turn)
            for p, term in enumerate((qr * gr + qi * gi, qr * gi - qi * gr, (qr * qr + qi * qi) * live)):
                probe_rows[p] += pltpu.roll(term, back, 1)

        pairs = size // 2
        found, value = [None] * pairs, [None] * pairs
        for step in range(pairs + 6):
            for stage in range(7):
                pair = step - stage
                if not 0 <= pair < pairs:
                    continue
                if stage == 0:
                    found[pair] = [find(begin + 2 * pair + j) for j in range(2)]
                    value[pair] = [exit_wave(slot) for slot in found[pair]]
                elif stage in (1, 4):
                    value[pair] = along_columns(value[pair], split_tables[stage // 4])
                elif stage in (2, 5):
                    value[pair] = along_rows(value[pair], split_tables[1 - stage // 4])
                elif stage == 3:
                    value[pair] = [scaled(slot, z) for slot, z in zip(found[pair], value[pair])]
                else:
                    for slot, g in zip(found[pair], value[pair]):
                        add(slot, g)

    def body(k, carry):
        work(k * BLOCK, BLOCK)
        return carry

    whole = (count + BLOCK // 2 - 1) // BLOCK
    lax.fori_loop(0, whole, body, 0)
    pl.when(count > whole * BLOCK)(lambda: work(whole * BLOCK, BLOCK // 2))
    outs = [pltpu.make_async_copy(sums.at[k], out_hbm.at[:, k], out_sem.at[k]) for k in range(STILES)]
    outs.append(pltpu.make_async_copy(probe_sums, sums_out, out_sem.at[STILES]))
    for copy in outs:
        copy.start()
    for copy in outs:
        copy.wait()


GRAIN = 4
VMEM_BYTES = 20 * 1024 * 1024
ANY = pl.BlockSpec(memory_space=pl.ANY)
VMEM = pl.BlockSpec(memory_space=pltpu.VMEM)


def dma(*shape):
    return pltpu.SemaphoreType.DMA(shape)


def sweep(iteration, strip, probe, old_sums, offsets, amplitudes, amplitudes_in, tables):
    cap = offsets[0].shape[1]
    updates = old_sums is not None
    return pl.pallas_call(
        functools.partial(sweep_kernel, iteration, updates),
        out_shape=(
            jax.ShapeDtypeStruct((GROUPS, STILES, 8, WIN), f32),
            jax.ShapeDtypeStruct((PTILES, 8, WIN), f32),
            jax.ShapeDtypeStruct(probe.shape, f32),
        ),
        in_specs=[ANY] * 12,
        out_specs=(ANY, ANY, VMEM),
        scratch_shapes=[pltpu.SMEM(array.shape, jnp.int32) for array in offsets]
        + [
            pltpu.VMEM(tables.shape, f32),
            pltpu.VMEM((2, 4 * WIN, 2 * WIN), jnp.bfloat16),
            pltpu.VMEM(probe.shape, f32),
            pltpu.VMEM((PTILES, 8, WIN), f32),
            pltpu.VMEM((OTILES, GROUPS, 8, WIN), f32),
            pltpu.VMEM((STILES, GROUPS, 8, WIN), f32),
            pltpu.VMEM((cap, WIN, WIN), f32),
            pltpu.VMEM((PTILES, 8, WIN), f32),
            dma(10),
            dma(OTILES),
            dma(2, cap // 2 // GRAIN),
            dma(STILES + 1),
        ],
        compiler_params=pltpu.CompilerParams(vmem_limit_bytes=VMEM_BYTES),
        name="sweep",
    )(*offsets, probe, old_sums if updates else probe, tables, strip, amplitudes, amplitudes_in)


class Place:
    def __init__(self):
        pos = lax.axis_index("pos")
        self.tile = lax.axis_index("tile")
        core, y, x = pos % 2, pos // 2 % RING, pos // (2 * RING)
        self.core, self.x, self.y = core, x, y
        self.near, self.far = x + core * (y - x), y + core * (x - y)
        self.near_step, self.far_step = 8 - 6 * core, 2 + 6 * core

    def at(self, near, far):
        return (self.near + near) % RING * self.near_step + (self.far + far) % RING * self.far_step + self.core

    def other_at(self, near, far):
        return (self.far + near) % RING * self.far_step + (self.near + far) % RING * self.near_step + 1 - self.core

    def x_peer(self, k):
        return {"pos": (self.x + k) % RING * 8 + self.y * 2 + self.core}

    def y_peer(self, k):
        return {"pos": self.x * 8 + (self.y + k) % RING * 2 + self.core}

    def near_peer(self, k):
        return {"pos": self.at(k, 0)}

    def far_peer(self, k):
        return {"pos": self.at(0, k)}

    def other(self):
        return {"pos": self.other_at(0, 0)}

    def tile_peer(self, k, tiles):
        return {"tile": (self.tile + k) % tiles}


def greet(place, tiles):
    barrier = pltpu.get_barrier_semaphore()
    peers = [place.other()] + [place.near_peer(k) for k in AWAY] + [place.far_peer(k) for k in AWAY]
    peers += [place.tile_peer(k, tiles) for k in range(1, tiles)]
    for peer in peers:
        pl.semaphore_signal(barrier, inc=1, device_id=peer, device_id_type=MESH)
    pl.semaphore_wait(barrier, len(peers))


class Sender:
    def __init__(self, send_sem, recv_sem):
        self.send_sem, self.recv_sem = send_sem, recv_sem
        self.names, self.sent = {}, []

    def copy(self, name, src, dst, device):
        k = self.names.setdefault(name, len(self.names))
        return pltpu.make_async_remote_copy(
            src_ref=src, dst_ref=dst, send_sem=self.send_sem.at[k], recv_sem=self.recv_sem.at[k],
            device_id=device, device_id_type=MESH)

    def send(self, name, src, dst, device):
        copy = self.copy(name, src, dst, device)
        copy.start()
        self.sent.append(copy)

    def arrive(self, name, dst, device):
        self.copy(name, dst, dst, device).wait_recv()

    def finish(self):
        for copy in self.sent:
            copy.wait_send()


class Reduce:
    def __init__(self, place, sender, src, own, core_in, far_in, near_in, load_sem, relay=False):
        self.place, self.sender, self.src, self.own = place, sender, src, own
        self.core_in, self.far_in, self.near_in, self.load_sem = core_in, far_in, near_in, load_sem
        self.loads = {}

    def load(self):
        for far in ALL:
            for near in ALL:
                copy = pltpu.make_async_copy(
                    self.src.at[pl.ds(2 * self.place.at(near, far), 2)], self.own.at[:, near, far],
                    self.load_sem.at[4 * near + far])
                copy.start()
                self.loads[near, far] = copy

    def core_send(self, h):
        for far in ALL:
            for near in ALL:
                self.sender.send(("core", h, near, far), self.src.at[2 * self.place.other_at(near, far) + h],
                                 self.core_in.at[h, near, far], self.place.other())

    def pair(self, h, near, far):
        copy = self.loads.pop((near, far), None)
        if copy is not None:
            copy.wait()
        self.sender.arrive(("core", h, near, far), self.core_in.at[h, near, far], self.place.other())
        self.own[h, near, far] += self.core_in[h, near, far]

    def far_send(self, h, fars=AWAY):
        for far in fars:
            for near in ALL:
                self.pair(h, near, far)
                self.sender.send(("far", h, near, far), self.own.at[h, near, far], self.far_in.at[h, far - 1, near],
                                 self.place.far_peer(far))

    relay_in = None

    def far_first(self, h):
        for near in ALL:
            self.pair(h, near, 2)
            for k, far in enumerate((1, 3)):
                part = pl.ds(k * STILES // 2, STILES // 2)
                self.sender.send(("relay", h, near, far), self.own.at[h, near, 2, part], self.relay_in.at[h, k, near],
                                 self.place.far_peer(far))

    def far_second(self, h):
        for near in ALL:
            for k, far in enumerate((1, 3)):
                self.pair(h, near, far)
                part = pl.ds(k * STILES // 2, STILES // 2)
                at = self.relay_in.at[h, k, near]
                self.sender.arrive(("relay", h, near, far), at, self.place.far_peer(RING - far))
                self.own[h, near, far, part] += at[...]
                self.sender.send(("far", h, near, far), self.own.at[h, near, far], self.far_in.at[h, far - 1, near],
                                 self.place.far_peer(far))

    def line(self, h, near):
        self.pair(h, near, 0)
        total = self.own[h, near, 0]
        for far in (1, 3) if self.relay_in is not None else (1, 3, 2):
            at = self.far_in.at[h, far - 1, near]
            self.sender.arrive(("far", h, near, far), at, self.place.far_peer(RING - far))
            total = total + at[...]
        self.own[h, near, 0] = total

    def near_send(self, h):
        for near in AWAY:
            self.line(h, near)
            self.sender.send(("near", h, near), self.own.at[h, near, 0], self.near_in.at[h, near - 1],
                             self.place.near_peer(near))

    def total(self, h):
        self.line(h, 0)
        total = self.own[h, 0, 0]
        for near in (1, 3, 2):
            at = self.near_in.at[h, near - 1]
            self.sender.arrive(("near", h, near), at, self.place.near_peer(RING - near))
            total = total + at[...]
        return total


class Gather:
    def __init__(self, place, sender, buf, name="o"):
        self.place, self.sender, self.buf, self.name = place, sender, buf, name

    def at(self, h, near, far):
        return self.buf.at[2 * self.place.at(near, far) + h]

    def spread(self, h, near):
        for far in (1, 3) if near in self.relays else AWAY:
            self.sender.send((self.name, "far", h, near, far), self.at(h, near, 0), self.at(h, near, 0), self.place.far_peer(far))

    def to_core(self, h, near, far):
        self.sender.send((self.name, "core", h, near, far), self.at(h, near, far), self.at(h, near, far), self.place.other())

    def start(self, h):
        for near in AWAY:
            self.sender.send((self.name, "near", h, near), self.at(h, 0, 0), self.at(h, 0, 0), self.place.near_peer(near))
        self.spread(h, 0)
        self.to_core(h, 0, 0)

    relays = ()

    def half(self, h, near, far, k):
        return self.buf.at[2 * self.place.at(near, far) + h, pl.ds(4 * k, 4)]

    def relay(self, h, near):
        for k, far in enumerate((1, 3)):
            back = RING - far
            self.sender.arrive((self.name, "far", h, near, far), self.at(h, near, back), self.place.far_peer(back))
            at = self.half(h, near, back, k)
            self.sender.send((self.name, "relay", h, near, far), at, at, self.place.far_peer(far))
            self.to_core(h, near, back)

    def relayed(self, h, near):
        for k, far in enumerate((1, 3)):
            self.sender.arrive((self.name, "relay", h, near, far), self.half(h, near, 2, k), self.place.far_peer(RING - far))
        self.to_core(h, near, 2)

    def middle(self, h):
        for near in (1, 3, 2):
            self.sender.arrive((self.name, "near", h, RING - near), self.at(h, near, 0), self.place.near_peer(near))
            self.spread(h, near)
        for near in (1, 3, 2):
            self.to_core(h, near, 0)

    def end(self, h, nears=(0, 1, 3, 2)):
        for near in self.relays:
            self.relay(h, near)
        for near in nears:
            if near in self.relays:
                continue
            for far in (1, 3, 2):
                self.sender.arrive((self.name, "far", h, near, RING - far), self.at(h, near, far), self.place.far_peer(far))
                self.to_core(h, near, far)

    def done(self, h):
        for near in self.relays:
            self.relayed(h, near)
        for near in range(RING):
            for far in range(RING):
                at = self.buf.at[2 * self.place.other_at(near, far) + h]
                self.sender.arrive((self.name, "core", h, near, far), at, self.place.other())


class ProbeSum:
    def __init__(self, place, sender, src, tiles, own, core_in, tile_in, x_in, y_in, total, load_sem):
        self.place, self.sender, self.src, self.tiles, self.own, self.core_in = place, sender, src, tiles, own, core_in
        self.tile_in, self.x_in, self.y_in, self.total, self.load_sem = tile_in, x_in, y_in, total, load_sem
        self.half = PTILES // 2
        self.part = self.half // tiles

    def tiles_of(self, core):
        return pl.ds(core * self.half, self.half)

    def load(self):
        self.copy = pltpu.make_async_copy(self.src.at[self.tiles_of(self.place.core)], self.own, self.load_sem)
        self.copy.start()

    def core(self):
        self.sender.send("core", self.src.at[self.tiles_of(1 - self.place.core)], self.core_in, self.place.other())

    def across(self):
        place = self.place
        self.copy.wait()
        self.sender.arrive("core", self.core_in, place.other())
        self.own[...] += self.core_in[...]
        for k in range(1, self.tiles):
            src = self.own.at[pl.ds((place.tile + k) % self.tiles * self.part, self.part)]
            self.sender.send(("tile", k), src, self.tile_in.at[k - 1], place.tile_peer(k, self.tiles))

    def spread(self, name, buf, at, peer):
        for k in AWAY:
            self.sender.send((name, k), buf.at[at], buf.at[at], peer(k))

    def collect(self, name, buf, at, peer):
        for k in (1, 3, 2):
            self.sender.arrive((name, k), buf.at[(at + RING - k) % RING], peer(RING - k))
        return (buf[0] + buf[1]) + (buf[2] + buf[3])

    def along_x(self):
        place = self.place
        total = self.own[pl.ds(place.tile * self.part, self.part)]
        for k in range(1, self.tiles):
            self.sender.arrive(("tile", k), self.tile_in.at[k - 1], place.tile_peer(self.tiles - k, self.tiles))
            total = total + self.tile_in[k - 1]
        self.x_in[place.x] = total
        self.spread("x", self.x_in, place.x, place.x_peer)

    def along_y(self):
        place = self.place
        self.y_in[place.y] = self.collect("x", self.x_in, place.x, place.x_peer)
        self.spread("y", self.y_in, place.y, place.y_peer)

    def share(self, tile):
        return self.total.at[pl.ds(self.place.core * self.half + tile * self.part, self.part)]

    def back(self):
        place = self.place
        at = self.share(place.tile)
        at[...] = self.collect("y", self.y_in, place.y, place.y_peer)
        for k in range(1, self.tiles):
            self.sender.send(("back", k), at, at, place.tile_peer(k, self.tiles))

    def back_core(self):
        place = self.place
        for k in range(1, self.tiles):
            source = (place.tile + self.tiles - k) % self.tiles
            self.sender.arrive(("back", k), self.share(source), {"tile": source})
        at = self.total.at[self.tiles_of(place.core)]
        self.sender.send("other", at, at, place.other())

    def finish(self):
        self.sender.arrive("other", self.total.at[self.tiles_of(1 - self.place.core)], self.place.other())
        return self.total


def gather_kernel(
    object_hbm, amp_hbm, rows_hbm, cols_hbm, counts_hbm, out_hbm, amp_in, rows_in, cols_in, counts_in,
    object_ref, mine, send_sem, recv_sem, copy_sem,
):
    place = Place()
    copy = pltpu.make_async_copy(object_hbm, object_ref, copy_sem)
    copy.start()
    copy.wait()
    for g in range(2):
        for p in range(2):
            for b in range(COLS):
                mine[g, COLS * p + b] = object_ref[p, 8 * g : 8 * g + 8, WIN * b : WIN * b + WIN]
    copy = pltpu.make_async_copy(mine, out_hbm.at[pl.ds(2 * place.at(0, 0), 2)], copy_sem)
    copy.start()
    greet(place, 1)
    copy.wait()
    sender = Sender(send_sem, recv_sem)
    strip = Gather(place, sender, out_hbm)
    strip.start(0)
    strip.start(1)
    other = place.other()
    moves = [(counts_hbm, counts_in), (rows_hbm, rows_in), (cols_hbm, cols_in)]
    moves += [(amp_hbm.at[k, :, 1 - place.core], amp_in.at[k]) for k in range(amp_in.shape[0])]
    for k, (src, dst) in enumerate(moves):
        sender.send(("move", k), src, dst, other)
    for h in range(2):
        strip.middle(h)
    for h in range(2):
        strip.end(h)
    for h in range(2):
        strip.done(h)
    for k, (_, dst) in enumerate(moves):
        sender.arrive(("move", k), dst, other)
    sender.finish()


def exchange_kernel(
    tiles, last, sums_hbm, probe_src, strip_hbm, *refs,
):
    if last:
        probe_ref, object_out, probe_out = refs[:3]
        refs = refs[3:]
    else:
        out_hbm, sums_out = refs[:2]
        refs = refs[2:]
    (old, own, core_in, far_in, near_in, relay_in, mine,
     p_own, p_core, p_tile, p_x, p_y, p_total,
     load_sem, copy_sem, send_sem, recv_sem, send_sem2, recv_sem2, send_sem3, recv_sem3) = refs
    place = Place()
    here = pl.ds(2 * place.at(0, 0), 2)
    load = pltpu.make_async_copy(strip_hbm.at[here], old, copy_sem.at[0])
    load.start()
    first, second, third = Sender(send_sem, recv_sem), Sender(send_sem2, recv_sem2), Sender(send_sem3, recv_sem3)
    sums = Reduce(place, first, sums_hbm, own, core_in, far_in, near_in, load_sem)
    sums.relay_in = relay_in
    probe = ProbeSum(
        place, third, probe_src, tiles, p_own, p_core, p_tile, p_x, p_y, p_total, copy_sem.at[3]
    )
    probe.load()
    sums.load()
    greet(place, tiles)
    probe.core()
    sums.core_send(0)
    sums.core_send(1)
    sums.far_first(0)
    probe.across()
    sums.far_first(1)
    sums.far_second(0)
    probe.along_x()
    sums.far_second(1)
    sums.near_send(0)
    probe.along_y()
    sums.near_send(1)
    strip = None if last else Gather(place, second, out_hbm)

    def step(h):
        total = sums.total(h)
        if h == 0:
            load.wait()
        for b in range(COLS):
            scale = 1.0 / (total[2 * COLS + b] + 1.0)
            for p in range(2):
                tile = (old[h, COLS * p + b] + total[COLS * p + b]) * scale
                if last:
                    object_out[p, 8 * h : 8 * h + 8, WIN * b : WIN * b + WIN] = tile
                else:
                    mine[h, COLS * p + b] = tile
        if not last:
            copy = pltpu.make_async_copy(mine.at[h], strip.at(h, 0, 0), copy_sem.at[1 + h])
            copy.start()
            copy.wait()
            strip.start(h)

    probe.back()
    step(0)
    step(1)
    probe.back_core()
    if last:
        stepped = probe_step(probe_ref, probe.finish().reshape(3, WIN, WIN))
        for k in range(2):
            probe_out[k] = stepped[k]
    else:
        for h in range(2):
            strip.middle(h)
        sums_out[...] = probe.finish()[...]
        for h in range(2):
            strip.end(h)
        for h in range(2):
            strip.done(h)
    for sender in (first, second, third):
        sender.finish()


def params(collective_id):
    return pltpu.CompilerParams(collective_id=collective_id, has_side_effects=True, vmem_limit_bytes=VMEM_BYTES)


GATHER_COPIES, REDUCE_COPIES = 62, 70


def gather_object(object_field, amplitudes, offsets):
    copies = GATHER_COPIES + 3 + amplitudes.shape[0]
    halves = amplitudes.shape[:2] + amplitudes.shape[3:]
    return pl.pallas_call(
        gather_kernel,
        out_shape=[jax.ShapeDtypeStruct((GROUPS, OTILES, 8, WIN), f32), jax.ShapeDtypeStruct(halves, f32)]
        + [jax.ShapeDtypeStruct(array.shape, jnp.int32) for array in offsets],
        in_specs=[ANY] * 5,
        out_specs=[ANY] * 5,
        scratch_shapes=[
            pltpu.VMEM(object_field.shape, f32), pltpu.VMEM((2, OTILES, 8, WIN), f32), dma(copies), dma(copies), pltpu.SemaphoreType.DMA,
        ],
        compiler_params=params(0),
        name="gather_object",
    )(object_field, amplitudes, *offsets)


def exchange(sums, probe_sums, strip, probe, object_shape):
    tiles = lax.axis_size("tile")
    is_last = probe is not None
    if is_last:
        out_shape = (jax.ShapeDtypeStruct(object_shape, f32), jax.ShapeDtypeStruct(probe.shape, f32))
        out_specs = (VMEM, VMEM)
    else:
        out_shape = (jax.ShapeDtypeStruct(strip.shape, f32), jax.ShapeDtypeStruct((PTILES, 8, WIN), f32))
        out_specs = (ANY, VMEM)
    group, part = (STILES, 8, WIN), (PTILES // 2 // tiles, 8, WIN)
    buffers = [
        (2, OTILES, 8, WIN), (2, RING, RING) + group, (2, RING, RING) + group, (2, 3, RING) + group, (2, 3) + group,
        (2, 2, RING, STILES // 2, 8, WIN), (2, OTILES, 8, WIN),
        (PTILES // 2, 8, WIN), (PTILES // 2, 8, WIN), (tiles - 1,) + part, (RING,) + part, (RING,) + part, (PTILES, 8, WIN),
    ]
    return pl.pallas_call(
        functools.partial(exchange_kernel, tiles, is_last),
        out_shape=out_shape,
        in_specs=[ANY, ANY, ANY] + ([VMEM] if is_last else []),
        out_specs=out_specs,
        scratch_shapes=[pltpu.VMEM(shape, f32) for shape in buffers]
        + [dma(RING * RING), dma(4)]
        + [dma(REDUCE_COPIES)] * 2 + [dma(GATHER_COPIES)] * 2 + [dma(8 + 2 * (tiles - 1))] * 2,
        compiler_params=params(2 if is_last else 1),
        name="exchange_last" if is_last else "exchange_middle",
    )(sums, probe_sums, strip, *([probe] if is_last else []))


def per_device(object_field, illumination, row_offsets, col_offsets, counts, amplitudes):
    tables = jnp.asarray(transform_tables())
    offsets = [row_offsets, col_offsets, counts.T]
    iterations, cap = row_offsets.shape
    amplitudes = amplitudes.reshape(iterations, cap // 2, 2, WIN, WIN)
    first, probe, tables, amplitudes, *offsets = (
        pltpu.with_memory_space_constraint(array, pltpu.HBM)
        for array in [object_field, illumination, tables, amplitudes, *offsets]
    )
    strip, amplitudes_in, *offsets_in = gather_object(first, amplitudes, offsets)
    old_sums = None
    for iteration in range(iterations):
        sums, probe_sums, probe = sweep(
            iteration, strip, probe, old_sums, offsets + offsets_in, amplitudes, amplitudes_in, tables
        )
        if iteration + 1 < iterations:
            strip, old_sums = exchange(sums, probe_sums, strip, None, None)
    return exchange(sums, probe_sums, strip, probe, object_field.shape)


def solution(mesh):
    return jax.shard_map(
        per_device,
        mesh=mesh,
        in_specs=(
            P(None, "pos", "tile"),
            P(),
            P(None, ("tile", "pos")),
            P(None, ("tile", "pos")),
            P(None, ("tile", "pos")),
            P(None, ("tile", "pos"), None, None),
        ),
        out_specs=(P(None, "pos", "tile"), P()),
        check_vma=False,
    )
```

```python
import functools
import math

import jax
import jax.numpy as jnp
import ml_dtypes
import numpy as np
from jax import lax
from jax.experimental import pallas as pl
from jax.experimental.pallas import tpu as pltpu
from jax.sharding import PartitionSpec as P

WIN = 128
ROWS = 512
GROUPS = ROWS // 8
COLS = ROWS // WIN
PTILES = 3 * WIN // 8
OTILES, STILES = 2 * COLS, 3 * COLS
BLOCK = 8
RING = 4
AWAY, ALL = (2, 1, 3), (2, 1, 3, 0)
MESH = pl.DeviceIdType.MESH
f32 = jnp.float32


def transform_tables():
    ramp = np.arange(WIN)
    angle = -2.0 * np.pi / WIN * (np.outer(ramp, ramp) % WIN)
    c, s = np.cos(angle) / math.sqrt(WIN), np.sin(angle) / math.sqrt(WIN)
    return np.stack([np.block([[c, s], [-s, c]]), np.block([[c, -s], [s, c]])]).astype(np.float32)


def split(x):
    high = x.astype(jnp.bfloat16)
    return high, (x - high.astype(f32)).astype(jnp.bfloat16)


def blocks(rows):
    halves = [[split(part) for part in row] for row in rows]
    return [jnp.concatenate([jnp.concatenate([part[k] for part in row], 1) for row in halves], 0) for k in range(2)]


def dot(a, b):
    return jnp.dot(a, b, preferred_element_type=f32)


def along_columns(pairs, table):
    high, low = blocks(pairs)
    both = dot(jnp.concatenate([high, low], 0), table[: 2 * WIN])
    return both[: 2 * WIN] + both[2 * WIN :] + dot(high, table[2 * WIN :])


def along_rows(y, table):
    quarter = [[y[j * WIN : (j + 1) * WIN, p * WIN : (p + 1) * WIN] for j in range(2)] for p in range(2)]
    high, low = blocks(quarter)
    both = dot(table, high)
    z = both[: 2 * WIN] + both[2 * WIN :] + dot(table[: 2 * WIN], low)
    return [(z[:WIN, j * WIN : (j + 1) * WIN], z[WIN:, j * WIN : (j + 1) * WIN]) for j in range(2)]


def probe_step(probe, sums):
    scale = lax.rsqrt(sums[2] + 1.0)
    return [probe[k] + (sums[k] - probe[k] * sums[2]) * scale for k in range(2)]


def sweep_kernel(
    iteration, updates,
    rows_hbm, cols_hbm, counts_hbm, rows_in, cols_in, counts_in, probe_hbm, old_hbm, tables_hbm, strip,
    amp_hbm, amp_in, sums, probe_sums, probe_out,
    rows, cols, counts, rows2, cols2, counts2, tables, split_tables, probe, old_sums, amp, small_sem, amp_sem,
):
    half = amp.shape[0] // 2
    core = lax.axis_index("pos") % 2
    small = [
        (counts_hbm, counts), (counts_in, counts2), (rows_hbm, rows), (rows_in, rows2), (cols_hbm, cols),
        (cols_in, cols2), (probe_hbm, probe), (tables_hbm, tables),
    ]
    if updates:
        small.append((old_hbm, old_sums))
    copies = [pltpu.make_async_copy(src, dst, small_sem.at[k]) for k, (src, dst) in enumerate(small)]
    for source, src in enumerate((amp_hbm.at[iteration, :, core], amp_in.at[iteration])):
        copies.append(pltpu.make_async_copy(src, amp.at[pl.ds(source * half, half)], amp_sem.at[source]))
    for copy in copies:
        copy.start()
    sums_rows = sums.reshape(STILES, ROWS, WIN)
    strip_rows = strip.reshape(OTILES, ROWS, WIN)
    probe_rows = probe_sums.reshape(3, WIN, WIN)
    for k in range(STILES):
        sums_rows[k] = jnp.zeros((ROWS, WIN), f32)
    for k in range(3):
        probe_rows[k] = jnp.zeros((WIN, WIN), f32)
    for copy in copies:
        copy.wait()
    mine = (counts[0, iteration] + 1 - core) // 2
    count = mine + (counts2[0, iteration] + 1 - core) // 2
    if updates:
        stepped = probe_step(probe, old_sums.reshape(3, WIN, WIN))
        for k in range(2):
            probe[k] = stepped[k]
    probe_out[...] = probe[...]
    for k in range(2):
        split_tables[k, : 2 * WIN], split_tables[k, 2 * WIN :] = split(tables[k])
    lane = lax.broadcasted_iota(jnp.int32, (WIN, WIN), 1)

    def work(begin, size):
        def find(number):
            theirs = number >= mine
            place = jnp.minimum(jnp.where(theirs, number - mine, number), half - 1)
            slot = 2 * place + core
            row = jnp.where(theirs, rows2[iteration, slot], rows[iteration, slot])
            col = jnp.where(theirs, cols2[iteration, slot], cols[iteration, slot])
            first, turn = col // WIN, col % WIN
            second = jnp.minimum(first + 1, COLS - 1)
            return number, jnp.where(theirs, half + place, place), pl.ds(row, WIN), first, second, turn

        def window(found):
            _, _, row, first, second, turn = found
            here = lane >= turn
            q = [
                jnp.where(here, strip_rows[COLS * p + first, row, :], strip_rows[COLS * p + second, row, :])
                for p in range(2)
            ]
            return here, q, [pltpu.roll(probe[p], turn, 1) for p in range(2)]

        def exit_wave(found):
            _, (qr, qi), (pr, pi) = window(found)
            return pr * qr - pi * qi, pr * qi + pi * qr

        def scaled(found, z):
            number, place = found[:2]
            re, im = z
            factor = amp[place] * lax.rsqrt(re * re + im * im + 1.0)
            factor = jnp.where(number < count, factor, 0.0)
            return re * factor, im * factor

        def add(found, g):
            number, _, row, first, second, turn = found
            here, (qr, qi), (pr, pi) = window(found)
            gr, gi = g
            live = (number < count).astype(f32)
            for p, term in enumerate((pr * gr + pi * gi, pr * gi - pi * gr, (pr * pr + pi * pi) * live)):
                sums_rows[COLS * p + first, row, :] += jnp.where(here, term, 0.0)
                sums_rows[COLS * p + second, row, :] += jnp.where(here, 0.0, term)
            back = jnp.where(turn == 0, 0, WIN - turn)
            for p, term in enumerate((qr * gr + qi * gi, qr * gi - qi * gr, (qr * qr + qi * qi) * live)):
                probe_rows[p] += pltpu.roll(term, back, 1)

        pairs = size // 2
        found, value = [None] * pairs, [None] * pairs
        for step in range(pairs + 6):
            for stage in range(7):
                pair = step - stage
                if not 0 <= pair < pairs:
                    continue
                if stage == 0:
                    found[pair] = [find(begin + 2 * pair + j) for j in range(2)]
                    value[pair] = [exit_wave(slot) for slot in found[pair]]
                elif stage in (1, 4):
                    value[pair] = along_columns(value[pair], split_tables[stage // 4])
                elif stage in (2, 5):
                    value[pair] = along_rows(value[pair], split_tables[1 - stage // 4])
                elif stage == 3:
                    value[pair] = [scaled(slot, z) for slot, z in zip(found[pair], value[pair])]
                else:
                    for slot, g in zip(found[pair], value[pair]):
                        add(slot, g)

    def body(k, carry):
        work(k * BLOCK, BLOCK)
        return carry

    whole = (count + BLOCK // 2 - 1) // BLOCK
    lax.fori_loop(0, whole, body, 0)
    pl.when(count > whole * BLOCK)(lambda: work(whole * BLOCK, BLOCK // 2))


VMEM_BYTES = 20 * 1024 * 1024
ANY = pl.BlockSpec(memory_space=pl.ANY)
VMEM = pl.BlockSpec(memory_space=pltpu.VMEM)


def dma(*shape):
    return pltpu.SemaphoreType.DMA(shape)


def sweep(iteration, strip, probe, old_sums, offsets, amplitudes, amplitudes_in, tables):
    cap = offsets[0].shape[1]
    updates = old_sums is not None
    return pl.pallas_call(
        functools.partial(sweep_kernel, iteration, updates),
        out_shape=(
            jax.ShapeDtypeStruct((STILES, GROUPS, 8, WIN), f32),
            jax.ShapeDtypeStruct((PTILES, 8, WIN), f32),
            jax.ShapeDtypeStruct(probe.shape, f32),
        ),
        in_specs=[ANY] * 9 + [VMEM] + [ANY] * 2,
        out_specs=(VMEM, VMEM, VMEM),
        scratch_shapes=[pltpu.SMEM(array.shape, jnp.int32) for array in offsets]
        + [
            pltpu.VMEM(tables.shape, f32),
            pltpu.VMEM((2, 4 * WIN, 2 * WIN), jnp.bfloat16),
            pltpu.VMEM(probe.shape, f32),
            pltpu.VMEM((PTILES, 8, WIN), f32),
            pltpu.VMEM((cap, WIN, WIN), f32),
            dma(10),
            dma(2),
        ],
        compiler_params=pltpu.CompilerParams(vmem_limit_bytes=VMEM_BYTES),
        name="sweep",
    )(*offsets, probe, old_sums if updates else probe, tables, strip, amplitudes, amplitudes_in)


class Place:
    def __init__(self):
        pos = lax.axis_index("pos")
        self.tile = lax.axis_index("tile")
        core, y, x = pos % 2, pos // 2 % RING, pos // (2 * RING)
        self.core, self.x, self.y = core, x, y
        self.near, self.far = x + core * (y - x), y + core * (x - y)
        self.near_step, self.far_step = 8 - 6 * core, 2 + 6 * core

    def at(self, near, far):
        return (self.near + near) % RING * self.near_step + (self.far + far) % RING * self.far_step + self.core

    def other_at(self, near, far):
        return (self.far + near) % RING * self.far_step + (self.near + far) % RING * self.near_step + 1 - self.core

    def x_peer(self, k):
        return {"pos": (self.x + k) % RING * 8 + self.y * 2 + self.core}

    def y_peer(self, k):
        return {"pos": self.x * 8 + (self.y + k) % RING * 2 + self.core}

    def near_peer(self, k):
        return {"pos": self.at(k, 0)}

    def far_peer(self, k):
        return {"pos": self.at(0, k)}

    def other(self):
        return {"pos": self.other_at(0, 0)}

    def tile_peer(self, k, tiles):
        return {"tile": (self.tile + k) % tiles}


def greet(place, tiles):
    barrier = pltpu.get_barrier_semaphore()
    peers = [place.other()] + [place.near_peer(k) for k in AWAY] + [place.far_peer(k) for k in AWAY]
    peers += [place.tile_peer(k, tiles) for k in range(1, tiles)]
    for peer in peers:
        pl.semaphore_signal(barrier, inc=1, device_id=peer, device_id_type=MESH)
    pl.semaphore_wait(barrier, len(peers))


class Sender:
    def __init__(self, send_sem, recv_sem):
        self.send_sem, self.recv_sem = send_sem, recv_sem
        self.names, self.sent = {}, []

    def copy(self, name, src, dst, device):
        k = self.names.setdefault(name, len(self.names))
        return pltpu.make_async_remote_copy(
            src_ref=src, dst_ref=dst, send_sem=self.send_sem.at[k], recv_sem=self.recv_sem.at[k],
            device_id=device, device_id_type=MESH)

    def send(self, name, src, dst, device):
        copy = self.copy(name, src, dst, device)
        copy.start()
        self.sent.append(copy)

    def arrive(self, name, dst, device):
        self.copy(name, dst, dst, device).wait_recv()

    def finish(self):
        for copy in self.sent:
            copy.wait_send()


class Reduce:
    def __init__(self, place, sender, src, own, core_in, far_in, near_in, load_sem, relay=False):
        self.place, self.sender, self.src, self.own = place, sender, src, own
        self.core_in, self.far_in, self.near_in, self.load_sem = core_in, far_in, near_in, load_sem
        self.loads = {}

    def load(self):
        for far in ALL:
            for near in ALL:
                for h in range(2):
                    src = self.src.at[:, 2 * self.place.at(near, far) + h]
                    sem = self.load_sem.at[2 * (4 * near + far) + h]
                    copy = pltpu.make_async_copy(src, self.own.at[h, near, far], sem)
                    copy.start()
                    self.loads[h, near, far] = copy

    def core_send(self, h):
        for far in ALL:
            for near in ALL:
                self.sender.send(("core", h, near, far), self.src.at[:, 2 * self.place.other_at(near, far) + h],
                                 self.core_in.at[h, near, far], self.place.other())

    def pair(self, h, near, far):
        self.loads[h, near, far].wait()
        self.sender.arrive(("core", h, near, far), self.core_in.at[h, near, far], self.place.other())
        self.own[h, near, far] += self.core_in[h, near, far]

    def far_send(self, h, fars=AWAY):
        for far in fars:
            for near in ALL:
                self.pair(h, near, far)
                self.sender.send(("far", h, near, far), self.own.at[h, near, far], self.far_in.at[h, far - 1, near],
                                 self.place.far_peer(far))

    relay_in = None

    def far_first(self, h):
        for near in ALL:
            self.pair(h, near, 2)
            for k, far in enumerate((1, 3)):
                part = pl.ds(k * STILES // 2, STILES // 2)
                self.sender.send(("relay", h, near, far), self.own.at[h, near, 2, part], self.relay_in.at[h, k, near],
                                 self.place.far_peer(far))

    def far_second(self, h):
        for near in ALL:
            for k, far in enumerate((1, 3)):
                self.pair(h, near, far)
                part = pl.ds(k * STILES // 2, STILES // 2)
                at = self.relay_in.at[h, k, near]
                self.sender.arrive(("relay", h, near, far), at, self.place.far_peer(RING - far))
                self.own[h, near, far, part] += at[...]
                self.sender.send(("far", h, near, far), self.own.at[h, near, far], self.far_in.at[h, far - 1, near],
                                 self.place.far_peer(far))

    def line(self, h, near):
        self.pair(h, near, 0)
        total = self.own[h, near, 0]
        for far in (1, 3) if self.relay_in is not None else (1, 3, 2):
            at = self.far_in.at[h, far - 1, near]
            self.sender.arrive(("far", h, near, far), at, self.place.far_peer(RING - far))
            total = total + at[...]
        self.own[h, near, 0] = total

    def near_send(self, h):
        for near in AWAY:
            self.line(h, near)
            self.sender.send(("near", h, near), self.own.at[h, near, 0], self.near_in.at[h, near - 1],
                             self.place.near_peer(near))

    def total(self, h):
        self.line(h, 0)
        total = self.own[h, 0, 0]
        for near in (1, 3, 2):
            at = self.near_in.at[h, near - 1]
            self.sender.arrive(("near", h, near), at, self.place.near_peer(RING - near))
            total = total + at[...]
        return total


class Gather:
    def __init__(self, place, sender, buf, name="o"):
        self.place, self.sender, self.buf, self.name = place, sender, buf, name

    def at(self, h, near, far):
        return self.buf.at[:, 2 * self.place.at(near, far) + h]

    def spread(self, h, near):
        for far in AWAY:
            self.sender.send((self.name, "far", h, near, far), self.at(h, near, 0), self.at(h, near, 0), self.place.far_peer(far))

    def to_core(self, h, near, far):
        self.sender.send((self.name, "core", h, near, far), self.at(h, near, far), self.at(h, near, far), self.place.other())

    def start(self, h):
        for near in AWAY:
            self.sender.send((self.name, "near", h, near), self.at(h, 0, 0), self.at(h, 0, 0), self.place.near_peer(near))
        self.spread(h, 0)
        self.to_core(h, 0, 0)

    def middle(self, h):
        for near in (1, 3, 2):
            self.sender.arrive((self.name, "near", h, RING - near), self.at(h, near, 0), self.place.near_peer(near))
            self.spread(h, near)
        for near in (1, 3, 2):
            self.to_core(h, near, 0)

    def end(self, h, nears=(0, 1, 3, 2)):
        for near in nears:
            for far in (1, 3, 2):
                self.sender.arrive((self.name, "far", h, near, RING - far), self.at(h, near, far), self.place.far_peer(far))
                self.to_core(h, near, far)

    def done(self, h):
        for near in range(RING):
            for far in range(RING):
                at = self.buf.at[:, 2 * self.place.other_at(near, far) + h]
                self.sender.arrive((self.name, "core", h, near, far), at, self.place.other())


class ProbeSum:
    def __init__(self, place, sender, src, tiles, own, core_in, tile_in, x_in, y_in, total, load_sem):
        self.place, self.sender, self.src, self.tiles, self.own, self.core_in = place, sender, src, tiles, own, core_in
        self.tile_in, self.x_in, self.y_in, self.total, self.load_sem = tile_in, x_in, y_in, total, load_sem
        self.half = PTILES // 2
        self.part = self.half // tiles

    def tiles_of(self, core):
        return pl.ds(core * self.half, self.half)

    def load(self):
        self.copy = pltpu.make_async_copy(self.src.at[self.tiles_of(self.place.core)], self.own, self.load_sem)
        self.copy.start()

    def core(self):
        self.sender.send("core", self.src.at[self.tiles_of(1 - self.place.core)], self.core_in, self.place.other())

    def across(self):
        place = self.place
        self.copy.wait()
        self.sender.arrive("core", self.core_in, place.other())
        self.own[...] += self.core_in[...]
        for k in range(1, self.tiles):
            src = self.own.at[pl.ds((place.tile + k) % self.tiles * self.part, self.part)]
            self.sender.send(("tile", k), src, self.tile_in.at[k - 1], place.tile_peer(k, self.tiles))

    def spread(self, name, buf, at, peer):
        for k in AWAY:
            self.sender.send((name, k), buf.at[at], buf.at[at], peer(k))

    def collect(self, name, buf, at, peer):
        for k in (1, 3, 2):
            self.sender.arrive((name, k), buf.at[(at + RING - k) % RING], peer(RING - k))
        return (buf[0] + buf[1]) + (buf[2] + buf[3])

    def along_x(self):
        place = self.place
        total = self.own[pl.ds(place.tile * self.part, self.part)]
        for k in range(1, self.tiles):
            self.sender.arrive(("tile", k), self.tile_in.at[k - 1], place.tile_peer(self.tiles - k, self.tiles))
            total = total + self.tile_in[k - 1]
        self.x_in[place.x] = total
        self.spread("x", self.x_in, place.x, place.x_peer)

    def along_y(self):
        place = self.place
        self.y_in[place.y] = self.collect("x", self.x_in, place.x, place.x_peer)
        self.spread("y", self.y_in, place.y, place.y_peer)

    def share(self, tile):
        return self.total.at[pl.ds(self.place.core * self.half + tile * self.part, self.part)]

    def back(self):
        place = self.place
        at = self.share(place.tile)
        at[...] = self.collect("y", self.y_in, place.y, place.y_peer)
        for k in range(1, self.tiles):
            self.sender.send(("back", k), at, at, place.tile_peer(k, self.tiles))

    def back_core(self):
        place = self.place
        for k in range(1, self.tiles):
            source = (place.tile + self.tiles - k) % self.tiles
            self.sender.arrive(("back", k), self.share(source), {"tile": source})
        at = self.total.at[self.tiles_of(place.core)]
        self.sender.send("other", at, at, place.other())

    def finish(self):
        self.sender.arrive("other", self.total.at[self.tiles_of(1 - self.place.core)], self.place.other())
        return self.total


def gather_kernel(
    object_hbm, amp_hbm, rows_hbm, cols_hbm, counts_hbm, out_hbm, amp_in, rows_in, cols_in, counts_in,
    object_ref, mine, send_sem, recv_sem, copy_sem,
):
    place = Place()
    copy = pltpu.make_async_copy(object_hbm, object_ref, copy_sem)
    copy.start()
    copy.wait()
    for g in range(2):
        for p in range(2):
            for b in range(COLS):
                mine[COLS * p + b, g] = object_ref[p, 8 * g : 8 * g + 8, WIN * b : WIN * b + WIN]
    copy = pltpu.make_async_copy(mine, out_hbm.at[:, pl.ds(2 * place.at(0, 0), 2)], copy_sem)
    copy.start()
    greet(place, 1)
    copy.wait()
    sender = Sender(send_sem, recv_sem)
    strip = Gather(place, sender, out_hbm)
    strip.start(0)
    strip.start(1)
    other = place.other()
    moves = [(counts_hbm, counts_in), (rows_hbm, rows_in), (cols_hbm, cols_in)]
    moves += [(amp_hbm.at[k, :, 1 - place.core], amp_in.at[k]) for k in range(amp_in.shape[0])]
    for k, (src, dst) in enumerate(moves):
        sender.send(("move", k), src, dst, other)
    for h in range(2):
        strip.middle(h)
    for h in range(2):
        strip.end(h)
    for h in range(2):
        strip.done(h)
    for k, (_, dst) in enumerate(moves):
        sender.arrive(("move", k), dst, other)
    sender.finish()


def exchange_kernel(
    tiles, last, sums_hbm, probe_src, strip_hbm, *refs,
):
    if last:
        probe_ref, object_out, probe_out = refs[:3]
        refs = refs[3:]
    else:
        out_hbm, sums_out = refs[:2]
        refs = refs[2:]
    (old, own, core_in, far_in, near_in, relay_in, mine,
     p_own, p_core, p_tile, p_x, p_y, p_total,
     load_sem, copy_sem, send_sem, recv_sem, send_sem2, recv_sem2, send_sem3, recv_sem3) = refs
    place = Place()
    here = pl.ds(2 * place.at(0, 0), 2)
    load = pltpu.make_async_copy(strip_hbm.at[:, here], old, copy_sem.at[0])
    load.start()
    first, second, third = Sender(send_sem, recv_sem), Sender(send_sem2, recv_sem2), Sender(send_sem3, recv_sem3)
    sums = Reduce(place, first, sums_hbm, own, core_in, far_in, near_in, load_sem)
    sums.relay_in = relay_in
    probe = ProbeSum(
        place, third, probe_src, tiles, p_own, p_core, p_tile, p_x, p_y, p_total, copy_sem.at[3]
    )
    probe.load()
    sums.load()
    greet(place, tiles)
    probe.core()
    sums.core_send(0)
    sums.core_send(1)
    sums.far_first(0)
    probe.across()
    sums.far_first(1)
    sums.far_second(0)
    probe.along_x()
    sums.far_second(1)
    sums.near_send(0)
    probe.along_y()
    sums.near_send(1)
    strip = None if last else Gather(place, second, out_hbm)

    def step(h):
        total = sums.total(h)
        if h == 0:
            load.wait()
        for b in range(COLS):
            scale = 1.0 / (total[2 * COLS + b] + 1.0)
            for p in range(2):
                tile = (old[COLS * p + b, h] + total[COLS * p + b]) * scale
                if last:
                    object_out[p, 8 * h : 8 * h + 8, WIN * b : WIN * b + WIN] = tile
                else:
                    mine[COLS * p + b, h] = tile
        if not last:
            copy = pltpu.make_async_copy(mine.at[:, h], strip.at(h, 0, 0), copy_sem.at[1 + h])
            copy.start()
            copy.wait()
            strip.start(h)

    probe.back()
    step(0)
    step(1)
    probe.back_core()
    if last:
        stepped = probe_step(probe_ref, probe.finish().reshape(3, WIN, WIN))
        for k in range(2):
            probe_out[k] = stepped[k]
    else:
        for h in range(2):
            strip.middle(h)
        sums_out[...] = probe.finish()[...]
        for h in range(2):
            strip.end(h)
        for h in range(2):
            strip.done(h)
    for sender in (first, second, third):
        sender.finish()


def params(collective_id):
    return pltpu.CompilerParams(collective_id=collective_id, has_side_effects=True, vmem_limit_bytes=VMEM_BYTES)


GATHER_COPIES, REDUCE_COPIES = 62, 70


def gather_object(object_field, amplitudes, offsets):
    copies = GATHER_COPIES + 3 + amplitudes.shape[0]
    halves = amplitudes.shape[:2] + amplitudes.shape[3:]
    return pl.pallas_call(
        gather_kernel,
        out_shape=[jax.ShapeDtypeStruct((OTILES, GROUPS, 8, WIN), f32), jax.ShapeDtypeStruct(halves, f32)]
        + [jax.ShapeDtypeStruct(array.shape, jnp.int32) for array in offsets],
        in_specs=[ANY] * 5,
        out_specs=[ANY] * 5,
        scratch_shapes=[
            pltpu.VMEM(object_field.shape, f32), pltpu.VMEM((OTILES, 2, 8, WIN), f32), dma(copies), dma(copies), pltpu.SemaphoreType.DMA,
        ],
        compiler_params=params(0),
        name="gather_object",
    )(object_field, amplitudes, *offsets)


def exchange(sums, probe_sums, strip, probe, object_shape):
    tiles = lax.axis_size("tile")
    is_last = probe is not None
    if is_last:
        out_shape = (jax.ShapeDtypeStruct(object_shape, f32), jax.ShapeDtypeStruct(probe.shape, f32))
        out_specs = (VMEM, VMEM)
    else:
        out_shape = (jax.ShapeDtypeStruct(strip.shape, f32), jax.ShapeDtypeStruct((PTILES, 8, WIN), f32))
        out_specs = (ANY, VMEM)
    group, part = (STILES, 8, WIN), (PTILES // 2 // tiles, 8, WIN)
    buffers = [
        (OTILES, 2, 8, WIN), (2, RING, RING) + group, (2, RING, RING) + group, (2, 3, RING) + group, (2, 3) + group,
        (2, 2, RING, STILES // 2, 8, WIN), (OTILES, 2, 8, WIN),
        (PTILES // 2, 8, WIN), (PTILES // 2, 8, WIN), (tiles - 1,) + part, (RING,) + part, (RING,) + part, (PTILES, 8, WIN),
    ]
    return pl.pallas_call(
        functools.partial(exchange_kernel, tiles, is_last),
        out_shape=out_shape,
        in_specs=[ANY, ANY, ANY] + ([VMEM] if is_last else []),
        out_specs=out_specs,
        scratch_shapes=[pltpu.VMEM(shape, f32) for shape in buffers]
        + [dma(2 * RING * RING), dma(4)]
        + [dma(REDUCE_COPIES)] * 2 + [dma(GATHER_COPIES)] * 2 + [dma(8 + 2 * (tiles - 1))] * 2,
        compiler_params=params(2 if is_last else 1),
        name="exchange_last" if is_last else "exchange_middle",
    )(sums, probe_sums, strip, *([probe] if is_last else []))


def per_device(object_field, illumination, row_offsets, col_offsets, counts, amplitudes):
    tables = jnp.asarray(transform_tables())
    offsets = [row_offsets, col_offsets, counts.T]
    iterations, cap = row_offsets.shape
    amplitudes = amplitudes.reshape(iterations, cap // 2, 2, WIN, WIN)
    first, probe, tables, amplitudes, *offsets = (
        pltpu.with_memory_space_constraint(array, pltpu.HBM)
        for array in [object_field, illumination, tables, amplitudes, *offsets]
    )
    strip, amplitudes_in, *offsets_in = gather_object(first, amplitudes, offsets)
    old_sums = None
    for iteration in range(iterations):
        sums, probe_sums, probe = sweep(
            iteration, strip, probe, old_sums, offsets + offsets_in, amplitudes, amplitudes_in, tables
        )
        if iteration + 1 < iterations:
            strip, old_sums = exchange(sums, probe_sums, strip, None, None)
    return exchange(sums, probe_sums, strip, probe, object_field.shape)


def solution(mesh):
    return jax.shard_map(
        per_device,
        mesh=mesh,
        in_specs=(
            P(None, "pos", "tile"),
            P(),
            P(None, ("tile", "pos")),
            P(None, ("tile", "pos")),
            P(None, ("tile", "pos")),
            P(None, ("tile", "pos"), None, None),
        ),
        out_specs=(P(None, "pos", "tile"), P()),
        check_vma=False,
    )
```

```python
import functools
import math

import jax
import jax.numpy as jnp
import ml_dtypes
import numpy as np
from jax import lax
from jax.experimental import pallas as pl
from jax.experimental.pallas import tpu as pltpu
from jax.sharding import PartitionSpec as P

WIN = 128
ROWS = 512
GROUPS = ROWS // 8
COLS = ROWS // WIN
PTILES = 3 * WIN // 8
OTILES, STILES = 2 * COLS, 3 * COLS
BLOCK = 8
RING = 4
AWAY, ALL = (2, 1, 3), (2, 1, 3, 0)
MESH = pl.DeviceIdType.MESH
f32 = jnp.float32


def transform_tables():
    ramp = np.arange(WIN)
    angle = -2.0 * np.pi / WIN * (np.outer(ramp, ramp) % WIN)
    c, s = np.cos(angle) / math.sqrt(WIN), np.sin(angle) / math.sqrt(WIN)
    return np.stack([np.block([[c, s], [-s, c]]), np.block([[c, -s], [s, c]])]).astype(np.float32)


def split(x):
    high = x.astype(jnp.bfloat16)
    return high, (x - high.astype(f32)).astype(jnp.bfloat16)


def blocks(rows):
    halves = [[split(part) for part in row] for row in rows]
    return [jnp.concatenate([jnp.concatenate([part[k] for part in row], 1) for row in halves], 0) for k in range(2)]


def dot(a, b):
    return jnp.dot(a, b, preferred_element_type=f32)


def along_columns(pairs, table):
    high, low = blocks(pairs)
    return dot(jnp.concatenate([high, high], 1), table) + dot(low, table[: 2 * WIN])


def along_rows(y, table):
    quarter = [[y[j * WIN : (j + 1) * WIN, p * WIN : (p + 1) * WIN] for j in range(2)] for p in range(2)]
    high, low = blocks(quarter)
    both = dot(table, high)
    z = both[: 2 * WIN] + both[2 * WIN :] + dot(table[: 2 * WIN], low)
    return [(z[:WIN, j * WIN : (j + 1) * WIN], z[WIN:, j * WIN : (j + 1) * WIN]) for j in range(2)]


def probe_step(probe, sums):
    scale = lax.rsqrt(sums[2] + 1.0)
    return [probe[k] + (sums[k] - probe[k] * sums[2]) * scale for k in range(2)]


def sweep_kernel(
    iteration, updates,
    rows_hbm, cols_hbm, counts_hbm, rows_in, cols_in, counts_in, probe_hbm, old_hbm, tables_hbm, strip,
    amp_hbm, amp_in, sums, probe_sums, probe_out,
    rows, cols, counts, rows2, cols2, counts2, tables, split_tables, probe, old_sums, power, amp, small_sem, amp_sem,
):
    half = amp.shape[0] // 2
    core = lax.axis_index("pos") % 2
    small = [
        (counts_hbm, counts), (counts_in, counts2), (rows_hbm, rows), (rows_in, rows2), (cols_hbm, cols),
        (cols_in, cols2), (probe_hbm, probe), (tables_hbm, tables),
    ]
    if updates:
        small.append((old_hbm, old_sums))
    copies = [pltpu.make_async_copy(src, dst, small_sem.at[k]) for k, (src, dst) in enumerate(small)]
    for source, src in enumerate((amp_hbm.at[iteration, :, core], amp_in.at[iteration])):
        copies.append(pltpu.make_async_copy(src, amp.at[pl.ds(source * half, half)], amp_sem.at[source]))
    for copy in copies:
        copy.start()
    sums_rows = sums.reshape(STILES, ROWS, WIN)
    strip_rows = strip.reshape(OTILES, ROWS, WIN)
    probe_rows = probe_sums.reshape(3, WIN, WIN)
    for k in range(STILES):
        sums_rows[k] = jnp.zeros((ROWS, WIN), f32)
    for k in range(3):
        probe_rows[k] = jnp.zeros((WIN, WIN), f32)
    for copy in copies:
        copy.wait()
    mine = (counts[0, iteration] + 1 - core) // 2
    count = mine + (counts2[0, iteration] + 1 - core) // 2
    if updates:
        stepped = probe_step(probe, old_sums.reshape(3, WIN, WIN))
        for k in range(2):
            probe[k] = stepped[k]
    probe_out[...] = probe[...]
    power[...] = probe[0] * probe[0] + probe[1] * probe[1]
    for k in range(2):
        split_tables[k, : 2 * WIN], split_tables[k, 2 * WIN :] = split(tables[k])
    lane = lax.broadcasted_iota(jnp.int32, (WIN, WIN), 1)

    def work(begin, size):
        windows = {}

        def find(number):
            theirs = number >= mine
            place = jnp.minimum(jnp.where(theirs, number - mine, number), half - 1)
            slot = 2 * place + core
            row = jnp.where(theirs, rows2[iteration, slot], rows[iteration, slot])
            col = jnp.where(theirs, cols2[iteration, slot], cols[iteration, slot])
            first, turn = col // WIN, col % WIN
            second = jnp.minimum(first + 1, COLS - 1)
            return number, jnp.where(theirs, half + place, place), pl.ds(row, WIN), first, second, turn

        def window(found):
            _, _, row, first, second, turn = found
            here = lane >= turn
            q = [
                jnp.where(here, strip_rows[COLS * p + first, row, :], strip_rows[COLS * p + second, row, :])
                for p in range(2)
            ]
            return here, q, [pltpu.roll(probe[p], turn, 1) for p in range(2)]

        def exit_wave(found):
            windows[id(found)] = window(found)
            _, (qr, qi), (pr, pi) = windows[id(found)]
            return pr * qr - pi * qi, pr * qi + pi * qr

        def scaled(found, z):
            number, place = found[:2]
            re, im = z
            factor = amp[place] * lax.rsqrt(re * re + im * im + 1.0)
            factor = jnp.where(number < count, factor, 0.0)
            return re * factor, im * factor

        def add(found, g):
            number, _, row, first, second, turn = found
            here, (qr, qi), (pr, pi) = windows[id(found)]
            gr, gi = g
            live = (number < count).astype(f32)
            for p, term in enumerate((pr * gr + pi * gi, pr * gi - pi * gr, (pltpu.roll(power[...], turn, 1)) * live)):
                sums_rows[COLS * p + first, row, :] += jnp.where(here, term, 0.0)
                sums_rows[COLS * p + second, row, :] += jnp.where(here, 0.0, term)
            back = jnp.where(turn == 0, 0, WIN - turn)
            for p, term in enumerate((qr * gr + qi * gi, qr * gi - qi * gr, (qr * qr + qi * qi) * live)):
                probe_rows[p] += pltpu.roll(term, back, 1)

        pairs = size // 2
        found, value = [None] * pairs, [None] * pairs
        for step in range(pairs + 6):
            for stage in range(7):
                pair = step - stage
                if not 0 <= pair < pairs:
                    continue
                if stage == 0:
                    found[pair] = [find(begin + 2 * pair + j) for j in range(2)]
                    value[pair] = [exit_wave(slot) for slot in found[pair]]
                elif stage in (1, 4):
                    value[pair] = along_columns(value[pair], split_tables[stage // 4])
                elif stage in (2, 5):
                    value[pair] = along_rows(value[pair], split_tables[1 - stage // 4])
                elif stage == 3:
                    value[pair] = [scaled(slot, z) for slot, z in zip(found[pair], value[pair])]
                else:
                    for slot, g in zip(found[pair], value[pair]):
                        add(slot, g)

    def body(k, carry):
        work(k * BLOCK, BLOCK)
        return carry

    whole = (count + BLOCK // 2 - 1) // BLOCK
    lax.fori_loop(0, whole, body, 0)
    pl.when(count > whole * BLOCK)(lambda: work(whole * BLOCK, BLOCK // 2))


VMEM_BYTES = 20 * 1024 * 1024
ANY = pl.BlockSpec(memory_space=pl.ANY)
VMEM = pl.BlockSpec(memory_space=pltpu.VMEM)


def dma(*shape):
    return pltpu.SemaphoreType.DMA(shape)


def sweep(iteration, strip, probe, old_sums, offsets, amplitudes, amplitudes_in, tables):
    cap = offsets[0].shape[1]
    updates = old_sums is not None
    return pl.pallas_call(
        functools.partial(sweep_kernel, iteration, updates),
        out_shape=(
            jax.ShapeDtypeStruct((STILES, GROUPS, 8, WIN), f32),
            jax.ShapeDtypeStruct((PTILES, 8, WIN), f32),
            jax.ShapeDtypeStruct(probe.shape, f32),
        ),
        in_specs=[ANY] * 9 + [VMEM] + [ANY] * 2,
        out_specs=(VMEM, VMEM, VMEM),
        scratch_shapes=[pltpu.SMEM(array.shape, jnp.int32) for array in offsets]
        + [
            pltpu.VMEM(tables.shape, f32),
            pltpu.VMEM((2, 4 * WIN, 2 * WIN), jnp.bfloat16),
            pltpu.VMEM(probe.shape, f32),
            pltpu.VMEM((PTILES, 8, WIN), f32),
            pltpu.VMEM((WIN, WIN), f32),
            pltpu.VMEM((cap, WIN, WIN), f32),
            dma(10),
            dma(2),
        ],
        compiler_params=pltpu.CompilerParams(vmem_limit_bytes=VMEM_BYTES),
        name="sweep",
    )(*offsets, probe, old_sums if updates else probe, tables, strip, amplitudes, amplitudes_in)


class Place:
    def __init__(self):
        pos = lax.axis_index("pos")
        self.tile = lax.axis_index("tile")
        core, y, x = pos % 2, pos // 2 % RING, pos // (2 * RING)
        self.core, self.x, self.y = core, x, y
        self.near, self.far = x + core * (y - x), y + core * (x - y)
        self.near_step, self.far_step = 8 - 6 * core, 2 + 6 * core

    def at(self, near, far):
        return (self.near + near) % RING * self.near_step + (self.far + far) % RING * self.far_step + self.core

    def other_at(self, near, far):
        return (self.far + near) % RING * self.far_step + (self.near + far) % RING * self.near_step + 1 - self.core

    def x_peer(self, k):
        return {"pos": (self.x + k) % RING * 8 + self.y * 2 + self.core}

    def y_peer(self, k):
        return {"pos": self.x * 8 + (self.y + k) % RING * 2 + self.core}

    def near_peer(self, k):
        return {"pos": self.at(k, 0)}

    def far_peer(self, k):
        return {"pos": self.at(0, k)}

    def other(self):
        return {"pos": self.other_at(0, 0)}

    def tile_peer(self, k, tiles, other):
        return {"tile": (self.tile + k) % tiles, "pos": self.other_at(0, 0) if other else self.at(0, 0)}


def greet(place, tiles):
    barrier = pltpu.get_barrier_semaphore()
    peers = [place.other()] + [place.near_peer(k) for k in AWAY] + [place.far_peer(k) for k in AWAY]
    peers += [place.tile_peer(k, tiles, other) for other in range(2) for k in range(1, tiles)]
    for peer in peers:
        pl.semaphore_signal(barrier, inc=1, device_id=peer, device_id_type=MESH)
    return lambda: pl.semaphore_wait(barrier, len(peers))


class Sender:
    def __init__(self, send_sem, recv_sem):
        self.send_sem, self.recv_sem = send_sem, recv_sem
        self.names, self.sent = {}, []

    def copy(self, name, src, dst, device):
        k = self.names.setdefault(name, len(self.names))
        return pltpu.make_async_remote_copy(
            src_ref=src, dst_ref=dst, send_sem=self.send_sem.at[k], recv_sem=self.recv_sem.at[k],
            device_id=device, device_id_type=MESH)

    def send(self, name, src, dst, device):
        copy = self.copy(name, src, dst, device)
        copy.start()
        self.sent.append(copy)

    def arrive(self, name, dst, device):
        self.copy(name, dst, dst, device).wait_recv()

    def finish(self):
        for copy in self.sent:
            copy.wait_send()


class Reduce:
    def __init__(self, place, sender, src, own, core_in, far_in, near_in, relay_in):
        self.place, self.sender, self.src, self.own = place, sender, src, own
        self.core_in, self.far_in, self.near_in, self.relay_in = core_in, far_in, near_in, relay_in

    def core_send(self, h):
        for far in ALL:
            for near in ALL:
                self.sender.send(("core", h, near, far), self.src.at[:, 2 * self.place.other_at(near, far) + h],
                                 self.core_in.at[h, near, far], self.place.other())

    def pair(self, h, near, far):
        self.sender.arrive(("core", h, near, far), self.core_in.at[h, near, far], self.place.other())
        mine = self.src[:, 2 * self.place.at(near, far) + h]
        self.own[h, near, far] = mine + self.core_in[h, near, far]

    def far_first(self, h):
        for near in ALL:
            self.pair(h, near, 2)
            for k, far in enumerate((1, 3)):
                part = pl.ds(k * STILES // 2, STILES // 2)
                self.sender.send(("relay", h, near, far), self.own.at[h, near, 2, part], self.relay_in.at[h, k, near],
                                 self.place.far_peer(far))

    def far_second(self, h):
        for near in ALL:
            for k, far in enumerate((1, 3)):
                self.pair(h, near, far)
                part = pl.ds(k * STILES // 2, STILES // 2)
                at = self.relay_in.at[h, k, near]
                self.sender.arrive(("relay", h, near, far), at, self.place.far_peer(RING - far))
                self.own[h, near, far, part] += at[...]
                self.sender.send(("far", h, near, far), self.own.at[h, near, far], self.far_in.at[h, far - 1, near],
                                 self.place.far_peer(far))

    def line(self, h, near):
        self.pair(h, near, 0)
        total = self.own[h, near, 0]
        for far in (1, 3):
            at = self.far_in.at[h, far - 1, near]
            self.sender.arrive(("far", h, near, far), at, self.place.far_peer(RING - far))
            total = total + at[...]
        self.own[h, near, 0] = total

    def near_send(self, h):
        for near in AWAY:
            self.line(h, near)
            self.sender.send(("near", h, near), self.own.at[h, near, 0], self.near_in.at[h, near - 1],
                             self.place.near_peer(near))

    def total(self, h):
        self.line(h, 0)
        total = self.own[h, 0, 0]
        for near in (1, 3, 2):
            at = self.near_in.at[h, near - 1]
            self.sender.arrive(("near", h, near), at, self.place.near_peer(RING - near))
            total = total + at[...]
        return total


class Gather:
    def __init__(self, place, sender, buf, name="o"):
        self.place, self.sender, self.buf, self.name = place, sender, buf, name

    def at(self, h, near, far):
        return self.buf.at[:, 2 * self.place.at(near, far) + h]

    def spread(self, h, near):
        for far in AWAY:
            self.sender.send((self.name, "far", h, near, far), self.at(h, near, 0), self.at(h, near, 0), self.place.far_peer(far))

    def to_core(self, h, near, far):
        self.sender.send((self.name, "core", h, near, far), self.at(h, near, far), self.at(h, near, far), self.place.other())

    def start(self, h):
        for near in AWAY:
            self.sender.send((self.name, "near", h, near), self.at(h, 0, 0), self.at(h, 0, 0), self.place.near_peer(near))
        self.spread(h, 0)
        self.to_core(h, 0, 0)

    def middle(self, h):
        for near in (1, 3, 2):
            self.sender.arrive((self.name, "near", h, RING - near), self.at(h, near, 0), self.place.near_peer(near))
            self.spread(h, near)
        for near in (1, 3, 2):
            self.to_core(h, near, 0)

    def end(self, h, nears=(0, 1, 3, 2)):
        for near in nears:
            for far in (1, 3, 2):
                self.sender.arrive((self.name, "far", h, near, RING - far), self.at(h, near, far), self.place.far_peer(far))
                self.to_core(h, near, far)

    def done(self, h):
        for near in range(RING):
            for far in range(RING):
                at = self.buf.at[:, 2 * self.place.other_at(near, far) + h]
                self.sender.arrive((self.name, "core", h, near, far), at, self.place.other())


class ProbeSum:
    def __init__(self, place, sender, src, tiles, tile_in, x_in, y_in, total):
        self.place, self.sender, self.src, self.tiles = place, sender, src, tiles
        self.tile_in, self.x_in, self.y_in, self.total = tile_in, x_in, y_in, total
        self.part = PTILES // 2 // tiles
        self.others = [(other, k) for k in range(tiles) for other in range(2) if other or k]

    def share(self, other, k):
        core = 1 - self.place.core if other else self.place.core
        return pl.ds(((self.place.tile + k) % self.tiles + core * self.tiles) * self.part, self.part)

    def peer(self, other, k):
        return self.place.tile_peer(k, self.tiles, other)

    def across(self):
        for other, k in self.others:
            src, dst = self.src.at[self.share(other, k)], self.tile_in.at[2 * k + other]
            self.sender.send(("tile", other, k), src, dst, self.peer(other, k))

    def spread(self, name, buf, at, peer):
        for k in AWAY:
            self.sender.send((name, k), buf.at[at], buf.at[at], peer(k))

    def collect(self, name, buf, at, peer):
        for k in (1, 3, 2):
            self.sender.arrive((name, k), buf.at[(at + RING - k) % RING], peer(RING - k))
        return (buf[0] + buf[1]) + (buf[2] + buf[3])

    def along_x(self):
        place = self.place
        total = self.src[self.share(0, 0)]
        for other, k in self.others:
            at = self.tile_in.at[2 * k + other]
            self.sender.arrive(("tile", other, k), at, self.peer(other, self.tiles - k))
            total = total + at[...]
        self.x_in[place.x] = total
        self.spread("x", self.x_in, place.x, place.x_peer)

    def along_y(self):
        place = self.place
        self.y_in[place.y] = self.collect("x", self.x_in, place.x, place.x_peer)
        self.spread("y", self.y_in, place.y, place.y_peer)

    def back(self):
        place = self.place
        at = self.total.at[self.share(0, 0)]
        at[...] = self.collect("y", self.y_in, place.y, place.y_peer)
        for other, k in self.others:
            self.sender.send(("back", other, k), at, at, self.peer(other, k))

    def finish(self):
        for other, k in self.others:
            back = self.tiles - k
            self.sender.arrive(("back", other, k), self.total.at[self.share(other, back)], self.peer(other, back))
        return self.total


def gather_kernel(
    object_hbm, amp_hbm, rows_hbm, cols_hbm, counts_hbm, out_ref, amp_in, rows_in, cols_in, counts_in,
    object_ref, send_sem, recv_sem, copy_sem,
):
    place = Place()
    met = greet(place, 1)
    copy = pltpu.make_async_copy(object_hbm, object_ref, copy_sem)
    copy.start()
    copy.wait()
    for g in range(2):
        for p in range(2):
            for b in range(COLS):
                out_ref[COLS * p + b, 2 * place.at(0, 0) + g] = object_ref[p, 8 * g : 8 * g + 8, WIN * b : WIN * b + WIN]
    met()
    sender = Sender(send_sem, recv_sem)
    strip = Gather(place, sender, out_ref)
    strip.start(0)
    strip.start(1)
    other = place.other()
    moves = [(counts_hbm, counts_in), (rows_hbm, rows_in), (cols_hbm, cols_in)]
    moves += [(amp_hbm.at[k, :, 1 - place.core], amp_in.at[k]) for k in range(amp_in.shape[0])]
    for k, (src, dst) in enumerate(moves):
        sender.send(("move", k), src, dst, other)
    for h in range(2):
        strip.middle(h)
    for h in range(2):
        strip.end(h)
    for h in range(2):
        strip.done(h)
    for k, (_, dst) in enumerate(moves):
        sender.arrive(("move", k), dst, other)
    sender.finish()


def exchange_kernel(
    tiles, last, sums_ref, probe_src, strip_ref, *refs,
):
    if last:
        probe_ref, object_out, probe_out = refs[:3]
        refs = refs[3:]
    else:
        out_ref, sums_out = refs[:2]
        refs = refs[2:]
    (own, core_in, far_in, near_in, relay_in,
     p_tile, p_x, p_y, p_total,
     send_sem, recv_sem, send_sem2, recv_sem2, send_sem3, recv_sem3) = refs
    place = Place()
    met = greet(place, tiles)
    first, second, third = Sender(send_sem, recv_sem), Sender(send_sem2, recv_sem2), Sender(send_sem3, recv_sem3)
    sums = Reduce(place, first, sums_ref, own, core_in, far_in, near_in, relay_in)
    probe = ProbeSum(place, third, probe_src, tiles, p_tile, p_x, p_y, p_total)
    met()
    probe.across()
    sums.core_send(0)
    sums.core_send(1)
    sums.far_first(0)
    sums.far_first(1)
    sums.far_second(0)
    probe.along_x()
    sums.far_second(1)
    sums.near_send(0)
    probe.along_y()
    sums.near_send(1)
    strip = None if last else Gather(place, second, out_ref)

    def step(h):
        total = sums.total(h)
        old = strip_ref[:, 2 * place.at(0, 0) + h]
        for b in range(COLS):
            scale = 1.0 / (total[2 * COLS + b] + 1.0)
            for p in range(2):
                tile = (old[COLS * p + b] + total[COLS * p + b]) * scale
                if last:
                    object_out[p, 8 * h : 8 * h + 8, WIN * b : WIN * b + WIN] = tile
                else:
                    out_ref[COLS * p + b, 2 * place.at(0, 0) + h] = tile
        if not last:
            strip.start(h)

    probe.back()
    step(0)
    step(1)
    if last:
        stepped = probe_step(probe_ref, probe.finish().reshape(3, WIN, WIN))
        for k in range(2):
            probe_out[k] = stepped[k]
    else:
        for h in range(2):
            strip.middle(h)
        sums_out[...] = probe.finish()[...]
        for h in range(2):
            strip.end(h)
        for h in range(2):
            strip.done(h)
    for sender in (first, second, third):
        sender.finish()


def params(collective_id):
    return pltpu.CompilerParams(collective_id=collective_id, has_side_effects=True, vmem_limit_bytes=VMEM_BYTES)


GATHER_COPIES, REDUCE_COPIES = 62, 70


def gather_object(object_field, amplitudes, offsets):
    copies = GATHER_COPIES + 3 + amplitudes.shape[0]
    halves = amplitudes.shape[:2] + amplitudes.shape[3:]
    return pl.pallas_call(
        gather_kernel,
        out_shape=[jax.ShapeDtypeStruct((OTILES, GROUPS, 8, WIN), f32), jax.ShapeDtypeStruct(halves, f32)]
        + [jax.ShapeDtypeStruct(array.shape, jnp.int32) for array in offsets],
        in_specs=[ANY] * 5,
        out_specs=[VMEM] + [ANY] * 4,
        scratch_shapes=[
            pltpu.VMEM(object_field.shape, f32), dma(copies), dma(copies), pltpu.SemaphoreType.DMA,
        ],
        compiler_params=params(0),
        name="gather_object",
    )(object_field, amplitudes, *offsets)


def exchange(sums, probe_sums, strip, probe, object_shape):
    tiles = lax.axis_size("tile")
    is_last = probe is not None
    if is_last:
        out_shape = (jax.ShapeDtypeStruct(object_shape, f32), jax.ShapeDtypeStruct(probe.shape, f32))
        out_specs = (VMEM, VMEM)
    else:
        out_shape = (jax.ShapeDtypeStruct(strip.shape, f32), jax.ShapeDtypeStruct((PTILES, 8, WIN), f32))
        out_specs = (VMEM, VMEM)
    group, part = (STILES, 8, WIN), (PTILES // 2 // tiles, 8, WIN)
    buffers = [
        (2, RING, RING) + group, (2, RING, RING) + group, (2, 3, RING) + group, (2, 3) + group,
        (2, 2, RING, STILES // 2, 8, WIN),
        (2 * tiles,) + part, (RING,) + part, (RING,) + part, (PTILES, 8, WIN),
    ]
    return pl.pallas_call(
        functools.partial(exchange_kernel, tiles, is_last),
        out_shape=out_shape,
        in_specs=[VMEM] * (4 if is_last else 3),
        out_specs=out_specs,
        scratch_shapes=[pltpu.VMEM(shape, f32) for shape in buffers]
        + [dma(REDUCE_COPIES)] * 2 + [dma(GATHER_COPIES)] * 2 + [dma(6 + 2 * (2 * tiles - 1))] * 2,
        compiler_params=params(2 if is_last else 1),
        name="exchange_last" if is_last else "exchange_middle",
    )(sums, probe_sums, strip, *([probe] if is_last else []))


def per_device(object_field, illumination, row_offsets, col_offsets, counts, amplitudes):
    tables = jnp.asarray(transform_tables())
    offsets = [row_offsets, col_offsets, counts.T]
    iterations, cap = row_offsets.shape
    amplitudes = amplitudes.reshape(iterations, cap // 2, 2, WIN, WIN)
    first, probe, tables, amplitudes, *offsets = (
        pltpu.with_memory_space_constraint(array, pltpu.HBM)
        for array in [object_field, illumination, tables, amplitudes, *offsets]
    )
    strip, amplitudes_in, *offsets_in = gather_object(first, amplitudes, offsets)
    old_sums = None
    for iteration in range(iterations):
        sums, probe_sums, probe = sweep(
            iteration, strip, probe, old_sums, offsets + offsets_in, amplitudes, amplitudes_in, tables
        )
        if iteration + 1 < iterations:
            strip, old_sums = exchange(sums, probe_sums, strip, None, None)
    return exchange(sums, probe_sums, strip, probe, object_field.shape)


def solution(mesh):
    return jax.shard_map(
        per_device,
        mesh=mesh,
        in_specs=(
            P(None, "pos", "tile"),
            P(),
            P(None, ("tile", "pos")),
            P(None, ("tile", "pos")),
            P(None, ("tile", "pos")),
            P(None, ("tile", "pos"), None, None),
        ),
        out_specs=(P(None, "pos", "tile"), P()),
        check_vma=False,
    )
```
